256 devices in a mesh: sta: 32 (over y, x, core), tm: 8 (over z).
Axes of the slice: x: 4, y: 4, z: 8, core: 2. Of those that a mesh axis runs over, the one named last changes fastest.
Arguments:
- traces: float32 [256, 65536], P('sta', 'tm'), may hold values from -100 to 100
- station_counts: int32 [32], P('sta'), may hold values from 4 to 8
- partners: int32 [32, 3], P('sta'), may hold values from -1 to 31, as said below
Outputs:
- correlations: float32 [32, 3, 8, 8, 1024], P('sta', None, None, None, 'tm')
The draws below stay inside these ranges and needn't reach their ends.
Inputs may be any that keep to these rules, and one draw needn't show every extreme that they name: partners[b, 0] = b; the other entries of row b are b plus distinct offsets between 1 and 3, or -1 where no pair block is listed.
All inputs are finite; a program needn't handle non-finite values.
Results may differ from the reference program's by a relative error of at most 0.0045.
Values may be sent and summed in bfloat16 or wider, within the bound.
A program may use at most 64 MiB of HBM per device.

```python
import math
import jax
import jax.numpy as jnp
from jax import lax

SB = 8
FREQ = 4096
BAND = 64
NLAG = 1024
REACH = 3
SLOTS = 3
BLOCKS = 32
STATIONS = 256
WINDOWS = 16
SAMPLES = 65536


def draw_traces(key, part):
    key = jax.random.fold_in(key, 1)
    noise_key, gain_key = jax.random.split(key)
    noise = jax.random.truncated_normal(noise_key, -5.0, 5.0, (STATIONS, SAMPLES), jnp.float32)
    gains = jnp.exp(jax.random.uniform(gain_key, (STATIONS, 1), jnp.float32, 0.0, math.log(10.0)))
    coeff = 0.9
    return gains * (noise + coeff * jnp.roll(noise, 1, axis=1))


def draw_partners(key, part):
    key = jax.random.fold_in(key, 2)
    score_key, keep_key = jax.random.split(key)
    scores = jax.random.randint(score_key, (BLOCKS, REACH), 0, 1 << 20)
    scores = scores * REACH + jnp.arange(REACH, dtype=jnp.int32)[None, :]
    order = jnp.argsort(scores, axis=1).astype(jnp.int32)
    offsets = order[:, :SLOTS - 1] + 1
    present = jax.random.randint(keep_key, (BLOCKS, SLOTS - 1), 0, 4) > 0
    block_ids = jnp.arange(BLOCKS, dtype=jnp.int32)[:, None]
    target = block_ids + offsets
    target = jnp.where(present & (target < BLOCKS), target, -1)
    return jnp.concatenate([block_ids, target], axis=1).astype(jnp.int32)


def with_ends(drawn, stream_key, smallest, top_value):
    longest = drawn.shape.index(max(drawn.shape))
    spots = []
    for shift in (0, 1):
        where = [jax.random.randint(jax.random.fold_in(stream_key, axis), (), 0, length) for axis, length in enumerate(drawn.shape)]
        where[longest] = (where[longest] + shift) % drawn.shape[longest]
        spots.append(tuple(where))
    return drawn.at[spots[0]].set(smallest).at[spots[1]].set(top_value)


def setup_inputs(seed: int = 0) -> dict:
    key_of = jax.random.split(jax.random.key(seed), 4)
    return {
        "traces": draw_traces(jax.random.fold_in(key_of[3], 71), 0),
        "station_counts": with_ends(jax.random.randint(key_of[1], (BLOCKS,), SB // 2, SB + 1), jax.random.fold_in(key_of[1], 1), SB // 2, SB).astype(jnp.int32),
        "partners": draw_partners(jax.random.fold_in(key_of[3], 71), 0),
    }


def reference(traces, station_counts, partners):
    hop_len = FREQ
    length = 2 * hop_len
    padded = jnp.concatenate([traces, jnp.zeros((STATIONS, hop_len), jnp.float32)], axis=1)
    halves = padded.reshape(STATIONS, WINDOWS + 1, hop_len)
    frames = jnp.concatenate([halves[:, :-1], halves[:, 1:]], axis=2)
    frames = frames - lax.optimization_barrier(jnp.mean(frames, axis=2, keepdims=True))
    sample_ids = jnp.arange(length, dtype=jnp.int32).astype(jnp.float32)
    taper = 0.5 - 0.5 * jnp.cos(sample_ids * (2.0 * math.pi / length))
    tapered = frames * taper
    spectrum = jnp.fft.rfft(tapered, axis=-1)[..., :hop_len]
    spec_re = jnp.real(spectrum)
    spec_im = jnp.imag(spectrum)
    power = (spec_re * spec_re + spec_im * spec_im).reshape(STATIONS, WINDOWS, hop_len // BAND, BAND)
    energy = lax.optimization_barrier(jnp.mean(power, axis=3, keepdims=True))
    scale = 1.0 / jnp.sqrt(energy + 1e-06)
    live = (jnp.arange(SB, dtype=jnp.int32)[None, :] < station_counts[:, None]).astype(jnp.float32)
    live = live.reshape(STATIONS, 1, 1, 1)
    white_re = (spec_re.reshape(STATIONS, WINDOWS, hop_len // BAND, BAND) * scale * live).astype(jnp.bfloat16)
    white_im = (spec_im.reshape(STATIONS, WINDOWS, hop_len // BAND, BAND) * scale * live).astype(jnp.bfloat16)
    block_re = white_re.reshape(BLOCKS, SB, WINDOWS, hop_len)
    block_im = white_im.reshape(BLOCKS, SB, WINDOWS, hop_len)
    norm = 1.0 / math.sqrt(2.0 * hop_len * WINDOWS)
    not_self = 1.0 - jnp.eye(SB, dtype=jnp.float32)

    def per_block(block_id):
        mine_re = lax.dynamic_index_in_dim(block_re, block_id, 0, False).astype(jnp.float32)
        mine_im = lax.dynamic_index_in_dim(block_im, block_id, 0, False).astype(jnp.float32)
        links = lax.dynamic_index_in_dim(partners, block_id, 0, False)
        results = []
        for slot_idx in range(SLOTS):
            target = links[slot_idx]
            valid = (target >= 0).astype(jnp.float32)
            safe = jnp.maximum(target, 0).astype(jnp.int32)
            other_re = lax.dynamic_index_in_dim(block_re, safe, 0, False).astype(jnp.float32) * valid
            other_im = lax.dynamic_index_in_dim(block_im, safe, 0, False).astype(jnp.float32) * valid
            cross_re = jnp.einsum('skf,tkf->stf', mine_re, other_re) + jnp.einsum('skf,tkf->stf', mine_im, other_im)
            cross_im = jnp.einsum('skf,tkf->stf', mine_im, other_re) - jnp.einsum('skf,tkf->stf', mine_re, other_im)
            if slot_idx == 0:
                cross_re = cross_re * not_self[:, :, None]
                cross_im = cross_im * not_self[:, :, None]
            full = lax.complex(cross_re, cross_im)
            full = jnp.concatenate([full, jnp.zeros((SB, SB, 1), full.dtype)], axis=2)
            series = jnp.fft.irfft(full, n=length, axis=-1) * (length * norm)
            results.append(jnp.concatenate([series[..., length - NLAG // 2:], series[..., :NLAG // 2]], axis=-1))
        return jnp.stack(results)
    return lax.map(per_block, jnp.arange(BLOCKS, dtype=jnp.int32))
```

```python
import functools
import math

import jax
import jax.numpy as jnp
import ml_dtypes
import numpy as np
from jax import lax
from jax.experimental import pallas as pl
from jax.experimental.pallas import tpu as pltpu
from jax.sharding import PartitionSpec as P

MESH = pl.DeviceIdType.MESH
F32 = jnp.float32
BF16 = jnp.bfloat16

ST = 8
FREQ = 4096
LENGTH = 2 * FREQ
BAND = 64
HALF_LAGS = 512
SLOTS = 3
REACH = 3
PAIRS = ST * ST
LIVE_ROWS = 33


def split(table):
    high = table.astype(ml_dtypes.bfloat16)
    low = (table - high.astype(np.float64)).astype(ml_dtypes.bfloat16)
    return np.stack([high, low])


def tables(window_count):
    m = np.arange(64)
    q = np.arange(128)
    taper = 0.5 - 0.5 * np.cos(np.arange(LENGTH) * (2.0 * math.pi / LENGTH))
    taper = np.repeat(taper.astype(np.float32).reshape(64, 1, 128), ST, axis=1)
    angle = 2.0 * math.pi * (np.outer(np.arange(LIVE_ROWS), m) % 64) / 64
    parts = np.concatenate([np.cos(angle), -np.sin(angle)])
    first = split(np.kron(parts, np.eye(ST)))
    angle = 2.0 * math.pi * np.outer(np.arange(64), q) / LENGTH
    turn = np.stack([np.cos(angle[:32]), np.sin(angle[:32]), np.cos(angle[32:]), np.sin(angle[32:])])
    turn = np.repeat(turn.astype(np.float32)[:, :, None, :], ST, axis=2)
    angle = 2.0 * math.pi * (np.outer(q, np.arange(BAND)) % 128) / 128
    cos, sin, none = np.cos(angle), np.sin(angle), np.zeros((128, BAND))
    second = np.concatenate(
        [
            np.concatenate([cos, none, -sin, none], axis=1),
            np.concatenate([sin, none, cos, none], axis=1),
            np.concatenate([none, cos, none, -sin], axis=1),
            np.concatenate([none, sin, none, cos], axis=1),
        ]
    )
    second = split(second)
    lane = np.arange(128)
    bins = 64 * (lane % 64)[None, :] + np.arange(32)[:, None] + 32 * (lane // 64)[None, :]
    angle = math.pi * bins / LENGTH
    shift = np.stack([np.cos(angle), np.sin(angle)]).astype(np.float32)
    shift = np.repeat(shift[:, :, None, :], ST, axis=2)
    order = bins.reshape(-1)
    weight = np.where(order == 0, 1.0, 2.0) / math.sqrt(LENGTH * window_count)
    steps = np.outer(order, 2 * np.arange(HALF_LAGS) + 1) % (2 * LENGTH)
    angle = math.pi * steps / LENGTH
    lag_cos = (weight[:, None] * np.cos(angle)).astype(ml_dtypes.bfloat16)
    lag_sin = (weight[:, None] * np.sin(angle)).astype(ml_dtypes.bfloat16)
    return taper, first, turn, second, shift, lag_cos, lag_sin


def kernel(
    n_sta,
    n_tm,
    x_hbm,
    counts,
    partners,
    tap_hbm,
    first_hbm,
    turn_hbm,
    second_hbm,
    shift_hbm,
    cos_hbm,
    sin_hbm,
    out_ref,
    xv,
    halo,
    tapv,
    firstv,
    turnv,
    secondv,
    shiftv,
    cosv,
    sinv,
    y,
    u,
    vhi,
    vlo,
    white,
    mine,
    got,
    cross0,
    cross12,
    part0,
    part12,
    recv0,
    recv12,
    load_sem,
    halo_sem,
    white_send,
    white_recv,
    p0_send,
    p0_recv,
    p12_send,
    p12_recv,
):
    b = lax.axis_index("sta")
    j = lax.axis_index("tm")
    lanes = 2 * HALF_LAGS // n_tm

    barrier = pltpu.get_barrier_semaphore()
    peers = [(b, lax.rem(j + d, n_tm)) for d in range(1, n_tm)]
    for d in range(1, REACH + 1):
        peers.append((lax.rem(b + d, n_sta), j))
        peers.append((lax.rem(b + n_sta - d, n_sta), j))
    for peer in peers:
        pl.semaphore_signal(barrier, inc=1, device_id=peer, device_id_type=MESH)

    loads = []
    for idx, (src, dst) in enumerate(
        [
            (x_hbm, xv),
            (tap_hbm, tapv),
            (first_hbm, firstv),
            (turn_hbm, turnv),
            (second_hbm, secondv),
            (shift_hbm, shiftv),
            (cos_hbm, cosv),
            (sin_hbm, sinv),
        ]
    ):
        copy = pltpu.make_async_copy(src, dst, load_sem.at[idx])
        copy.start()
        loads.append(copy)

    pl.semaphore_wait(barrier, len(peers))
    halo_copy = pltpu.make_async_remote_copy(
        src_ref=x_hbm.at[pl.ds(0, 32)],
        dst_ref=halo,
        send_sem=halo_sem.at[0],
        recv_sem=halo_sem.at[1],
        device_id=(b, lax.rem(j + n_tm - 1, n_tm)),
        device_id_type=MESH,
    )
    halo_copy.start()

    station = lax.broadcasted_iota(jnp.int32, (ST, 128), 0)
    live = (station < counts[0]).astype(F32)

    def first_step(frames):
        total = jnp.sum(jnp.sum(frames, axis=0), axis=1, keepdims=True)
        frames = (frames - (total * (1.0 / LENGTH))[None]) * tapv[...]
        frames = frames.reshape(64 * ST, 128)
        high = frames.astype(BF16)
        y[:, 0:128] = high
        y[:, 128:256] = (frames - high.astype(F32)).astype(BF16)
        both = jnp.dot(firstv[0], y[...], preferred_element_type=F32)
        u[...] = (
            both[:, 0:128]
            + both[:, 128:256]
            + jnp.dot(firstv[1], y[:, 0:128], preferred_element_type=F32)
        ).reshape(2 * LIVE_ROWS, ST, 128)

    def turned(row):
        re0, im0 = u[row], u[LIVE_ROWS + row]
        re1, im1 = u[32 - row], u[LIVE_ROWS + 32 - row]
        c0, s0, c1, s1 = turnv[0, row], turnv[1, row], turnv[2, row], turnv[3, row]
        return (
            re0 * c0 + im0 * s0,
            im0 * c0 - re0 * s0,
            re1 * c1 - im1 * s1,
            -(im1 * c1 + re1 * s1),
        )

    def second_step(w):
        for i in range(16):
            pair = zip(turned(2 * i), turned(2 * i + 1))
            for block, (upper, lower) in enumerate(pair):
                v = jnp.concatenate([upper, lower], axis=0)
                high = v.astype(BF16)
                vhi[16 * i : 16 * i + 16, 128 * block : 128 * block + 128] = high
                vlo[16 * i : 16 * i + 16, 128 * block : 128 * block + 128] = (
                    v - high.astype(F32)
                ).astype(BF16)
        spec = (
            jnp.dot(vhi[...], secondv[0], preferred_element_type=F32)
            + jnp.dot(vlo[...], secondv[0], preferred_element_type=F32)
            + jnp.dot(vhi[...], secondv[1], preferred_element_type=F32)
        )
        re = spec[:, 0:128].reshape(32, ST, 128)
        im = spec[:, 128:256].reshape(32, ST, 128)
        energy = jnp.sum(re * re + im * im, axis=0)
        energy = (energy + pltpu.roll(energy, 64, 1)) * (1.0 / BAND)
        scale = live / jnp.sqrt(energy + 1e-06)
        re = (re * scale[None]).reshape(256, 128).astype(BF16)
        im = (im * scale[None]).reshape(256, 128).astype(BF16)
        white[w, 0] = re
        white[w, 1] = im
        re = re.astype(F32).reshape(32, ST, 128)
        im = im.astype(F32).reshape(32, ST, 128)
        mine[w, 0] = re * shiftv[0] + im * shiftv[1]
        mine[w, 1] = im * shiftv[0] - re * shiftv[1]

    def send_white(w):
        copies = []
        for d in range(1, REACH + 1):
            copy = pltpu.make_async_remote_copy(
                src_ref=white.at[w],
                dst_ref=got.at[w, d - 1],
                send_sem=white_send.at[w, d - 1],
                recv_sem=white_recv.at[w, d - 1],
                device_id=(lax.rem(b + n_sta - d, n_sta), j),
                device_id_type=MESH,
            )
            copy.start()
            copies.append(copy)
        return copies

    for copy in loads[:6]:
        copy.wait()
    first_step(xv[...])
    second_step(0)
    sent = send_white(0)
    halo_copy.wait()
    inside = (j < n_tm - 1).astype(F32)
    first_step(jnp.concatenate([xv[32:64], halo[...] * inside], axis=0))
    second_step(1)
    sent += send_white(1)

    def cross_terms(others, cross, slots):
        def body(i, carry):
            rows = pl.ds(pl.multiple_of(16 * i, 16), 16)
            right = others(rows)
            for half in range(2):
                row = 2 * i + half
                at = pl.ds(pl.multiple_of(row * 128, 128), 128)
                part = slice(8 * half, 8 * half + 8)
                for s in range(0, ST, 2):
                    kept = [[], []]
                    for t in (s, s + 1):
                        left = [
                            [
                                jnp.broadcast_to(mine[w, c, row, t : t + 1, :], (ST, 128))
                                for c in range(2)
                            ]
                            for w in range(2)
                        ]
                        for slot in range(slots):
                            re, im = None, None
                            for w in range(2):
                                a_re, a_im = left[w]
                                o_re, o_im = (value[part] for value in right[slot][w])
                                new_re = a_re * o_re + a_im * o_im
                                new_im = a_im * o_re - a_re * o_im
                                re = new_re if re is None else re + new_re
                                im = new_im if im is None else im + new_im
                            kept[0].append(re)
                            kept[1].append(im)
                    for slot in range(slots):
                        at_rows = pl.ds(slot * PAIRS + s * ST, 16)
                        for c in range(2):
                            cross[c, at_rows, at] = jnp.concatenate(
                                [kept[c][slot], kept[c][slots + slot]], axis=0
                            ).astype(BF16)
            return carry

        lax.fori_loop(0, 16, body, 0)

    def lag_terms(cross, part):
        even = jnp.dot(cross[0], cosv[...], preferred_element_type=F32)
        odd = jnp.dot(cross[1], sinv[...], preferred_element_type=F32)
        later = even - odd
        earlier = even + odd
        for e in range(n_tm // 2):
            at = slice(lanes * e, lanes * e + lanes)
            part[n_tm // 2 + e] = later[:, at].astype(BF16)
            part[n_tm // 2 - 1 - e] = earlier[:, at].astype(BF16)

    def send_part(part, recv, send_sem, recv_sem):
        copies = []
        for d in range(1, n_tm):
            to = lax.rem(j + d, n_tm)
            copy = pltpu.make_async_remote_copy(
                src_ref=part.at[to],
                dst_ref=recv.at[d - 1],
                send_sem=send_sem.at[d - 1],
                recv_sem=recv_sem.at[d - 1],
                device_id=(b, to),
                device_id_type=MESH,
            )
            copy.start()
            copies.append(copy)
        return copies

    cross_terms(
        lambda rows: [[[white[w, c, rows, :].astype(F32) for c in range(2)] for w in range(2)]],
        cross0,
        1,
    )
    loads[6].wait()
    loads[7].wait()
    lag_terms(cross0, part0)
    terms0 = send_part(part0, recv0, p0_send, p0_recv)

    for copy in sent:
        copy.wait()
    takes = [
        [(partners[0, slot] == b + d).astype(F32) for d in range(1, REACH + 1)]
        for slot in range(1, SLOTS)
    ]

    def chosen(rows):
        slots = [[[None, None], [None, None]] for _ in takes]
        for w in range(2):
            for c in range(2):
                values = [got[w, d, c, rows, :].astype(F32) for d in range(REACH)]
                for slot, take in enumerate(takes):
                    slots[slot][w][c] = (
                        values[0] * take[0] + values[1] * take[1] + values[2] * take[2]
                    )
        return slots

    cross_terms(chosen, cross12, SLOTS - 1)
    lag_terms(cross12, part12)
    terms12 = send_part(part12, recv12, p12_send, p12_recv)

    row = lax.broadcasted_iota(jnp.int32, (lanes, lanes), 0)
    column = lax.broadcasted_iota(jnp.int32, (lanes, lanes), 1)
    wanted = jnp.where(j >= n_tm // 2, column, lanes - 1 - column)
    order = (row == wanted).astype(F32)

    def finish(part, recv, copies):
        total = part[j].astype(F32)
        for d, copy in enumerate(copies):
            copy.wait()
            total = total + recv[d].astype(F32)
        return jnp.dot(
            total, order, precision=lax.Precision.HIGHEST, preferred_element_type=F32
        )

    own = finish(part0, recv0, terms0)
    pair = lax.broadcasted_iota(jnp.int32, (PAIRS, lanes), 0)
    own = jnp.where((pair >> 3) == (pair & 7), 0.0, own)
    out_ref[0:PAIRS, :] = own
    out_ref[PAIRS : SLOTS * PAIRS, :] = finish(part12, recv12, terms12)


def shards(n_sta, n_tm, traces, station_counts, partners):
    x = traces.reshape(ST, 64, 128).transpose(1, 0, 2)
    consts = [jnp.asarray(table) for table in tables(2 * n_tm)]
    lanes = 2 * HALF_LAGS // n_tm
    anywhere = pl.BlockSpec(memory_space=pl.ANY)
    scalars = pl.BlockSpec(memory_space=pltpu.SMEM)
    dma = pltpu.SemaphoreType.DMA
    series = pl.pallas_call(
        functools.partial(kernel, n_sta, n_tm),
        out_shape=jax.ShapeDtypeStruct((SLOTS * PAIRS, lanes), F32),
        in_specs=[anywhere, scalars, scalars] + [anywhere] * len(consts),
        out_specs=pl.BlockSpec(memory_space=pltpu.VMEM),
        scratch_shapes=[
            pltpu.VMEM((64, ST, 128), F32),
            pltpu.VMEM((32, ST, 128), F32),
            *[pltpu.VMEM(table.shape, table.dtype) for table in consts],
            pltpu.VMEM((64 * ST, 256), BF16),
            pltpu.VMEM((2 * LIVE_ROWS, ST, 128), F32),
            pltpu.VMEM((256, 512), BF16),
            pltpu.VMEM((256, 512), BF16),
            pltpu.VMEM((2, 2, 256, 128), BF16),
            pltpu.VMEM((2, 2, 32, ST, 128), F32),
            pltpu.VMEM((2, REACH, 2, 256, 128), BF16),
            pltpu.VMEM((2, PAIRS, FREQ), BF16),
            pltpu.VMEM((2, 2 * PAIRS, FREQ), BF16),
            pltpu.VMEM((n_tm, PAIRS, lanes), BF16),
            pltpu.VMEM((n_tm, 2 * PAIRS, lanes), BF16),
            pltpu.VMEM((n_tm - 1, PAIRS, lanes), BF16),
            pltpu.VMEM((n_tm - 1, 2 * PAIRS, lanes), BF16),
            dma((8,)),
            dma((2,)),
            dma((2, REACH)),
            dma((2, REACH)),
            dma((n_tm - 1,)),
            dma((n_tm - 1,)),
            dma((n_tm - 1,)),
            dma((n_tm - 1,)),
        ],
        compiler_params=pltpu.CompilerParams(
            collective_id=0, has_side_effects=True, vmem_limit_bytes=56 * 2**20
        ),
    )(x, station_counts, partners, *consts)
    return series.reshape(1, SLOTS, ST, ST, lanes)


def solution(mesh):
    placed = (P("sta", "tm"), P("sta"), P("sta", None))
    return jax.shard_map(
        functools.partial(shards, mesh.shape["sta"], mesh.shape["tm"]),
        mesh=mesh,
        in_specs=placed,
        out_specs=P("sta", None, None, None, "tm"),
        check_vma=False,
    )
```

```python
import functools
import math

import jax
import jax.numpy as jnp
import ml_dtypes
import numpy as np
from jax import lax
from jax.experimental import pallas as pl
from jax.experimental.pallas import tpu as pltpu
from jax.sharding import PartitionSpec as P

MESH = pl.DeviceIdType.MESH
F32 = jnp.float32
BF16 = jnp.bfloat16

ST = 8
FREQ = 4096
LENGTH = 2 * FREQ
BAND = 64
HALF_LAGS = 512
SLOTS = 3
REACH = 3
PAIRS = ST * ST
VMEM_LIMIT = 55100 * 2**10
LIVE_ROWS = 33


def split(table):
    high = table.astype(ml_dtypes.bfloat16)
    low = (table - high.astype(np.float64)).astype(ml_dtypes.bfloat16)
    return np.stack([high, low])


def tables(parts):
    m = np.arange(64)
    q = np.arange(128)
    taper = 0.5 - 0.5 * np.cos(np.arange(LENGTH) * (2.0 * math.pi / LENGTH))
    taper = np.repeat(taper.astype(np.float32).reshape(64, 1, 128), ST, axis=1)
    angle = 2.0 * math.pi * (np.outer(np.arange(LIVE_ROWS), m) % 64) / 64
    first = split(np.kron(np.concatenate([np.cos(angle), -np.sin(angle)]), np.eye(ST)))
    ids = np.arange(32)
    mirrored = np.where(ids == 0, 32, 64 - ids)
    near = 2.0 * math.pi * np.outer(ids, q) / LENGTH
    far = 2.0 * math.pi * np.outer(mirrored, q) / LENGTH
    turn = np.stack([np.cos(near), np.sin(near), np.cos(far), np.sin(far)])
    turn = np.repeat(turn.astype(np.float32)[:, :, None, :], ST, axis=2)
    k = np.arange(BAND)
    angle = 2.0 * math.pi * (np.outer(q, k) % 128) / 128
    cos, sin, none = np.cos(angle), np.sin(angle), np.zeros((128, BAND))
    back_cos, back_sin = cos[:, ::-1], sin[:, ::-1]
    second = np.concatenate(
        [
            np.concatenate([cos, none, -sin, none], axis=1),
            np.concatenate([sin, none, cos, none], axis=1),
            np.concatenate([none, back_cos, none, -back_sin], axis=1),
            np.concatenate([none, back_sin, none, back_cos], axis=1),
        ]
    )
    second = split(second)
    bins = np.concatenate(
        [64 * k[None, :] + ids[:, None], 64 * (63 - k)[None, :] + mirrored[:, None]], axis=1
    )
    angle = math.pi * bins / LENGTH
    shift = np.stack([np.cos(angle), np.sin(angle)]).astype(np.float32)
    shift = np.repeat(shift[:, :, None, :], ST, axis=2)
    band = bins[0] // BAND
    same_band = (band[:, None] == band[None, :]).astype(np.float32)
    mirror = (bins[0][:, None] + bins[0][None, :] == FREQ).astype(np.float32)
    lane_maps = np.stack([same_band, mirror])
    order = bins.reshape(-1)
    lags = np.arange(HALF_LAGS).reshape(parts // 2, -1, 2).transpose(0, 2, 1).reshape(-1)
    steps = np.outer(order, 2 * lags + 1) % (2 * LENGTH)
    weight = np.where(order == 0, 1.0, 2.0)
    lag_cos = weight[:, None] * np.cos(math.pi * steps / LENGTH)
    lag_cos = lag_cos.reshape(FREQ, 2, 256).transpose(1, 0, 2).astype(ml_dtypes.bfloat16)
    return taper, first, turn, second, shift, lane_maps, lag_cos


def kernel(
    n_sta,
    n_tm,
    x_hbm,
    counts,
    partners,
    tap_hbm,
    first_hbm,
    turn_hbm,
    second_hbm,
    shift_hbm,
    maps_hbm,
    cos_hbm,
    out_ref,
    xv,
    halo,
    tapv,
    firstv,
    turnv,
    secondv,
    shiftv,
    mapsv,
    cosv,
    y,
    u,
    vhi,
    vlo,
    white,
    mine,
    got,
    cross0,
    cross12,
    held,
    part0,
    part12,
    recv0,
    recv12,
    load_sem,
    come,
    halo_sem,
    white_send,
    white_recv,
    p0_send,
    p0_recv,
    p12_send,
    p12_recv,
):
    b = lax.axis_index("sta")
    j = lax.axis_index("tm")
    lanes = 2 * HALF_LAGS // n_tm
    group = n_tm // 2

    barrier = pltpu.get_barrier_semaphore()
    neighbours = [(b, lax.rem(j + 1, n_tm)), (b, lax.rem(j + n_tm - 1, n_tm))]
    peers = list(neighbours)
    odd = lax.rem(b, 2)
    ahead = (lax.rem(b + 2, n_sta), j)
    behind = (lax.rem(b + n_sta - 2, n_sta), j)
    sibling = (b + 1 - 2 * odd, j)
    across = (lax.rem(b + n_sta - 3 + 6 * odd, n_sta), j)
    third = (lax.rem(b + n_sta - 3 + 2 * odd, n_sta), j)
    peers += [ahead, behind, sibling, across]
    for peer in peers:
        pl.semaphore_signal(barrier, inc=1, device_id=peer, device_id_type=MESH)

    def pass_on(step):
        for neighbour in neighbours:
            pl.semaphore_signal(
                come.at[step], inc=1, device_id=neighbour, device_id_type=MESH
            )

    loads = []
    for idx, (src, dst) in enumerate(
        [
            (x_hbm, xv),
            (tap_hbm, tapv),
            (first_hbm, firstv),
            (turn_hbm, turnv),
            (second_hbm, secondv),
            (shift_hbm, shiftv),
            (maps_hbm, mapsv),
            (cos_hbm, cosv),
        ]
    ):
        loads.append(pltpu.make_async_copy(src, dst, load_sem.at[idx]))
    for copy in loads[:-1]:
        copy.start()

    loads[0].wait()
    pl.semaphore_wait(barrier, len(peers))
    halo_copy = pltpu.make_async_remote_copy(
        src_ref=xv.at[pl.ds(0, 32)],
        dst_ref=halo,
        send_sem=halo_sem.at[0],
        recv_sem=halo_sem.at[1],
        device_id=(b, lax.rem(j + n_tm - 1, n_tm)),
        device_id_type=MESH,
    )
    halo_copy.start()
    pass_on(0)
    loads[-1].start()

    station = lax.broadcasted_iota(jnp.int32, (ST, 128), 0)
    live = (station < counts[0]).astype(F32)

    def exact_dot(a, b):
        return jnp.dot(a, b, precision=lax.Precision.HIGHEST, preferred_element_type=F32)

    def first_step(frames):
        total = jnp.sum(jnp.sum(frames, axis=0), axis=1, keepdims=True)
        frames = (frames - (total * (1.0 / LENGTH))[None]) * tapv[...]
        frames = frames.reshape(64 * ST, 128)
        high = frames.astype(BF16)
        y[:, 0:128] = high
        y[:, 128:256] = (frames - high.astype(F32)).astype(BF16)
        both = jnp.dot(firstv[0], y[...], preferred_element_type=F32)
        u[...] = (
            both[:, 0:128]
            + both[:, 128:256]
            + jnp.dot(firstv[1], y[:, 0:128], preferred_element_type=F32)
        ).reshape(2 * LIVE_ROWS, ST, 128)

    def turned(row):
        re0, im0 = u[row], u[LIVE_ROWS + row]
        re1, im1 = (u[32], u[LIVE_ROWS + 32]) if row == 0 else (re0, im0)
        c0, s0, c1, s1 = turnv[0, row], turnv[1, row], turnv[2, row], turnv[3, row]
        return (
            re0 * c0 + im0 * s0,
            im0 * c0 - re0 * s0,
            re1 * c1 - im1 * s1,
            -(im1 * c1 + re1 * s1),
        )

    def mirrored_bins(value):
        return jnp.concatenate([exact_dot(value[0], mapsv[1])[None], pltpu.roll(value[1:], 64, 2)])

    def second_step(w):
        for i in range(16):
            pair = zip(turned(2 * i), turned(2 * i + 1))
            for block, (upper, lower) in enumerate(pair):
                v = jnp.concatenate([upper, lower], axis=0)
                high = v.astype(BF16)
                vhi[16 * i : 16 * i + 16, 128 * block : 128 * block + 128] = high
                vlo[16 * i : 16 * i + 16, 128 * block : 128 * block + 128] = (
                    v - high.astype(F32)
                ).astype(BF16)
        spec = (
            jnp.dot(vhi[...], secondv[0], preferred_element_type=F32)
            + jnp.dot(vlo[...], secondv[0], preferred_element_type=F32)
            + jnp.dot(vhi[...], secondv[1], preferred_element_type=F32)
        )
        re = spec[:, 0:128].reshape(32, ST, 128)
        im = spec[:, 128:256].reshape(32, ST, 128)
        energy = exact_dot(jnp.sum(re * re + im * im, axis=0), mapsv[0]) * (1.0 / BAND)
        scale = live / jnp.sqrt(energy + 1e-06)
        re = (re * scale[None]).reshape(2, 128, 128).astype(BF16)
        im = (im * scale[None]).reshape(2, 128, 128).astype(BF16)
        for part in range(2):
            white[w, part, 0] = re[part]
            white[w, part, 1] = im[part]

    def shifted(w):
        re = white[w, :, 0].astype(F32).reshape(32, ST, 128)
        im = white[w, :, 1].astype(F32).reshape(32, ST, 128)
        left = (re * shiftv[0] + im * shiftv[1], im * shiftv[0] - re * shiftv[1])
        for c in range(2):
            mine[w, c] = left[c]
            mine[w, 2 + c] = mirrored_bins(left[c])

    def start_white(w, part, place, source, to):
        copy = pltpu.make_async_remote_copy(
            src_ref=source,
            dst_ref=got.at[w, part, place],
            send_sem=white_send.at[w, part, place],
            recv_sem=white_recv.at[w, part, place],
            device_id=to,
            device_id_type=MESH,
        )
        copy.start()
        return copy

    def send_white(w):
        near = [start_white(w, part, 0, white.at[w, part], behind) for part in range(2)]
        far = [start_white(w, part, 1, white.at[w, part], third) for part in range(2)]
        return [[near[part], far[part]] for part in range(2)]

    def hand_on(w, part, copies):
        copies[part][0].wait()
        copies[part].append(start_white(w, part, 2, got.at[w, part, 0], sibling))

    for copy in loads[1:-1]:
        copy.wait()
    first_step(xv[...])
    second_step(0)
    sent0 = send_white(0)
    pl.semaphore_wait(come.at[0], 2)
    pass_on(1)
    shifted(0)
    halo_copy.wait()
    inside = (j < n_tm - 1).astype(F32)
    first_step(jnp.concatenate([xv[32:64], halo[...] * inside], axis=0))
    second_step(1)
    sent1 = send_white(1)
    pl.semaphore_wait(come.at[1], 2)
    pass_on(2)
    shifted(1)

    def cross_pair(others, cross, slots, part, i, first):
        rows = pl.ds(i * 16, 16)
        right = others(part, rows)
        for half in range(2):
            row = 16 * part + 2 * i + half
            at = pl.ds(row * 128, 128)
            own = slice(8 * half, 8 * half + 8)
            terms = []
            for slot in range(slots):
                terms.append([])
                for w in range(2):
                    values = [right[slot][w][c][own] for c in range(2)]
                    if first and part == 0 and half == 0:
                        values += [
                            jnp.dot(
                                value.astype(BF16),
                                mapsv[1].astype(BF16),
                                preferred_element_type=F32,
                            )
                            for value in values
                        ]
                    else:
                        values += [pltpu.roll(value, 64, 1) for value in values]
                    terms[slot].append(values)
            for s in range(0, ST, 2):
                kept = [[], []]
                for t in (s, s + 1):
                    left = [
                        [
                            jnp.broadcast_to(mine[w, c, row, t : t + 1, :], (ST, 128))
                            for c in range(4)
                        ]
                        for w in range(2)
                    ]
                    for slot in range(slots):
                        re, im = None, None
                        for w in range(2):
                            a_re, a_im, back_re, back_im = left[w]
                            o_re, o_im, other_re, other_im = terms[slot][w]
                            new_re = a_re * o_re + a_im * o_im
                            new_im = back_im * other_re - back_re * other_im
                            re = new_re if re is None else re + new_re
                            im = new_im if im is None else im + new_im
                        kept[0].append(re - im)
                        kept[1].append(re + im)
                for slot in range(slots):
                    for sign in range(2):
                        at_rows = pl.ds((sign * slots + slot) * PAIRS + s * ST, 16)
                        cross[at_rows, at] = jnp.concatenate(
                            [kept[sign][slot], kept[sign][slots + slot]], axis=0
                        ).astype(BF16)

    def cross_terms(others, cross, slots, part):
        for i in range(8):
            cross_pair(others, cross, slots, part, i, i == 0)

    half_bins = FREQ // 2
    place = lax.rem(j + n_tm // 4, group)
    far_half = lax.div(lax.rem(j + n_tm // 4, n_tm), group)

    def lag_sums(cross, half, part):
        at = slice(half_bins * part, half_bins * part + half_bins)
        return jnp.dot(cross[:, at], cosv[half, at, :], preferred_element_type=F32)

    def keep_part(sums, half, part):
        rows = sums.shape[0] // 2
        lane = lax.broadcasted_iota(jnp.int32, (rows, 256), 1)
        even = lax.rem(lane, lanes) < lanes // 2
        minus, plus = sums[:rows], sums[rows:]
        later = jnp.where(even, minus, plus).astype(BF16)
        earlier = jnp.where(even, plus, minus).astype(BF16)
        for e in range(n_tm // 4):
            at = slice(lanes * e, lanes * e + lanes)
            block = half * (n_tm // 4) + e
            part[group + block] = later[:, at]
            part[group - 1 - block] = earlier[:, at]

    def send_part(part, recv, send_sem, recv_sem, far):
        copies = []
        for r in range(0 if far else 1, group):
            to = lax.rem(j + n_tm - place + lax.rem(place + r, group) + (group if far else 0), n_tm)
            idx = r if far else group + r - 1
            copy = pltpu.make_async_remote_copy(
                src_ref=part.at[to],
                dst_ref=recv.at[idx],
                send_sem=send_sem.at[idx],
                recv_sem=recv_sem.at[idx],
                device_id=(b, to),
                device_id_type=MESH,
            )
            copy.start()
            copies.append(copy)
        return copies

    def own_rows(part, rows):
        return [[[white[w, part, c, rows, :].astype(F32) for c in range(2)] for w in range(2)]]

    cross_terms(own_rows, cross0, 1, 0)
    hand_on(0, 0, sent0)
    hand_on(0, 1, sent0)
    cross_terms(own_rows, cross0, 1, 1)
    loads[-1].wait()
    pl.semaphore_wait(come.at[2], 2)
    terms0 = []
    for far in (True, False):
        half = far_half if far else 1 - far_half
        keep_part(lag_sums(cross0, half, 0) + lag_sums(cross0, half, 1), half, part0)
        terms0 += send_part(part0, recv0, p0_send, p0_recv, far)

    hand_on(1, 0, sent1)
    hand_on(1, 1, sent1)
    offsets = (2, 1 + 2 * odd, 3 - 2 * odd)
    takes = [
        [(partners[slot] == b + offset).astype(F32) for offset in offsets]
        for slot in range(1, SLOTS)
    ]

    def chosen(part, rows):
        slots = [[[None, None], [None, None]] for _ in takes]
        for w in range(2):
            for c in range(2):
                values = [got[w, part, d, c, rows, :].astype(F32) for d in range(REACH)]
                for slot, take in enumerate(takes):
                    slots[slot][w][c] = (
                        values[0] * take[0] + values[1] * take[1] + values[2] * take[2]
                    )
        return slots

    for part in range(2):
        for copy in sent0[part][1:] + sent1[part][1:]:
            copy.wait()
        cross_terms(chosen, cross12, SLOTS - 1, part)
        if part == 0:
            for half in range(2):
                held[half] = lag_sums(cross12, half, 0)
    terms12 = []
    for far in (True, False):
        half = far_half if far else 1 - far_half
        keep_part(held[half] + lag_sums(cross12, half, 1), half, part12)
        terms12 += send_part(part12, recv12, p12_send, p12_recv, far)

    row = lax.broadcasted_iota(jnp.int32, (lanes, lanes), 0)
    column = lax.broadcasted_iota(jnp.int32, (lanes, lanes), 1)
    lag = jnp.where(row < lanes // 2, 2 * row, 2 * row - lanes + 1)
    lag = jnp.where(j >= group, lag, lanes - 1 - lag)
    order = (lag == column).astype(F32)

    def finish(part, recv, copies):
        total = part[j].astype(F32)
        for idx in list(range(group, n_tm - 1)) + list(range(group)):
            copies[idx].wait()
            total = total + recv[idx].astype(F32)
        return exact_dot(total, order)

    own = finish(part0, recv0, terms0)
    pair = lax.broadcasted_iota(jnp.int32, (PAIRS, lanes), 0)
    own = jnp.where((pair >> 3) == (pair & 7), 0.0, own)
    out_ref[0:PAIRS, :] = own
    out_ref[PAIRS : SLOTS * PAIRS, :] = finish(part12, recv12, terms12)


def shards(n_sta, n_tm, traces, station_counts, partners):
    x = traces.reshape(ST, 64, 128).transpose(1, 0, 2)
    consts = [jnp.asarray(table) for table in tables(n_tm)]
    lanes = 2 * HALF_LAGS // n_tm
    anywhere = pl.BlockSpec(memory_space=pl.ANY)
    scalars = pl.BlockSpec(memory_space=pltpu.SMEM)
    dma = pltpu.SemaphoreType.DMA
    series = pl.pallas_call(
        functools.partial(kernel, n_sta, n_tm),
        out_shape=jax.ShapeDtypeStruct((SLOTS * PAIRS, lanes), F32),
        in_specs=[anywhere, scalars, scalars] + [anywhere] * len(consts),
        out_specs=pl.BlockSpec(memory_space=pltpu.VMEM),
        scratch_shapes=[
            pltpu.VMEM((64, ST, 128), F32),
            pltpu.VMEM((32, ST, 128), F32),
            *[pltpu.VMEM(table.shape, table.dtype) for table in consts],
            pltpu.VMEM((64 * ST, 256), BF16),
            pltpu.VMEM((2 * LIVE_ROWS, ST, 128), F32),
            pltpu.VMEM((256, 512), BF16),
            pltpu.VMEM((256, 512), BF16),
            pltpu.VMEM((2, 2, 2, 128, 128), BF16),
            pltpu.VMEM((2, 4, 32, ST, 128), F32),
            pltpu.VMEM((2, 2, REACH, 2, 128, 128), BF16),
            pltpu.VMEM((2 * PAIRS, FREQ), BF16),
            pltpu.VMEM((4 * PAIRS, FREQ), BF16),
            pltpu.VMEM((2, 4 * PAIRS, 256), F32),
            pltpu.VMEM((n_tm, PAIRS, lanes), BF16),
            pltpu.VMEM((n_tm, 2 * PAIRS, lanes), BF16),
            pltpu.VMEM((n_tm - 1, PAIRS, lanes), BF16),
            pltpu.VMEM((n_tm - 1, 2 * PAIRS, lanes), BF16),
            dma((8,)),
            pltpu.SemaphoreType.REGULAR((n_tm // 2 - 1,)),
            dma((2,)),
            dma((2, 2, REACH)),
            dma((2, 2, REACH)),
            dma((n_tm - 1,)),
            dma((n_tm - 1,)),
            dma((n_tm - 1,)),
            dma((n_tm - 1,)),
        ],
        compiler_params=pltpu.CompilerParams(
            collective_id=0, has_side_effects=True, vmem_limit_bytes=VMEM_LIMIT
        ),
    )(x, station_counts, partners.reshape(SLOTS), *consts)
    norm = 1.0 / math.sqrt(2.0 * LENGTH * n_tm)
    return (series * norm).reshape(1, SLOTS, ST, ST, lanes)


def solution(mesh):
    placed = (P("sta", "tm"), P("sta"), P("sta", None))
    return jax.shard_map(
        functools.partial(shards, mesh.shape["sta"], mesh.shape["tm"]),
        mesh=mesh,
        in_specs=placed,
        out_specs=P("sta", None, None, None, "tm"),
        check_vma=False,
    )
```

```python
import functools
import math

import jax
import jax.numpy as jnp
import ml_dtypes
import numpy as np
from jax import lax
from jax.experimental import pallas as pl
from jax.experimental.pallas import tpu as pltpu
from jax.sharding import PartitionSpec as P

MESH = pl.DeviceIdType.MESH
F32 = jnp.float32
BF16 = jnp.bfloat16

ST = 8
FREQ = 4096
LENGTH = 2 * FREQ
BAND = 64
HALF_LAGS = 512
SLOTS = 3
REACH = 3
PAIRS = ST * ST
VMEM_LIMIT = 55100 * 2**10
LIVE_ROWS = 33


def split(table):
    high = table.astype(ml_dtypes.bfloat16)
    low = (table - high.astype(np.float64)).astype(ml_dtypes.bfloat16)
    return np.stack([high, low])


def tables():
    m = np.arange(64)
    q = np.arange(128)
    taper = 0.5 - 0.5 * np.cos(np.arange(LENGTH) * (2.0 * math.pi / LENGTH))
    taper = np.repeat(taper.astype(np.float32).reshape(64, 1, 128), ST, axis=1)
    angle = 2.0 * math.pi * (np.outer(np.arange(LIVE_ROWS), m) % 64) / 64
    first = split(np.kron(np.concatenate([np.cos(angle), -np.sin(angle)]), np.eye(ST)))
    ids = np.arange(32)
    mirrored = np.where(ids == 0, 32, 64 - ids)
    near = 2.0 * math.pi * np.outer(ids, q) / LENGTH
    far = 2.0 * math.pi * np.outer(mirrored, q) / LENGTH
    turn = np.stack([np.cos(near), np.sin(near), np.cos(far), np.sin(far)])
    turn = np.repeat(turn.astype(np.float32)[:, :, None, :], ST, axis=2)
    k = np.arange(BAND)
    angle = 2.0 * math.pi * (np.outer(q, k) % 128) / 128
    cos, sin, none = np.cos(angle), np.sin(angle), np.zeros((128, BAND))
    back_cos, back_sin = cos[:, ::-1], sin[:, ::-1]
    second = np.concatenate(
        [
            np.concatenate([cos, none, -sin, none], axis=1),
            np.concatenate([sin, none, cos, none], axis=1),
            np.concatenate([none, back_cos, none, -back_sin], axis=1),
            np.concatenate([none, back_sin, none, back_cos], axis=1),
        ]
    )
    second = split(second)
    bins = np.concatenate(
        [64 * k[None, :] + ids[:, None], 64 * (63 - k)[None, :] + mirrored[:, None]], axis=1
    )
    angle = math.pi * bins / LENGTH
    shift = np.stack([np.cos(angle), np.sin(angle)]).astype(np.float32)
    shift = np.repeat(shift[:, :, None, :], ST, axis=2)
    order = bins.reshape(-1)
    steps = np.outer(order, 2 * np.arange(HALF_LAGS) + 1) % (2 * LENGTH)
    weight = np.where(order == 0, 1.0, 2.0)
    lag_cos = weight[:, None] * np.cos(math.pi * steps / LENGTH)
    lag_cos = lag_cos.reshape(FREQ, 2, 256).transpose(1, 0, 2).astype(ml_dtypes.bfloat16)
    return taper, first, turn, second, shift, lag_cos


def kernel(
    n_sta,
    n_tm,
    x_hbm,
    counts,
    partners,
    tap_hbm,
    first_hbm,
    turn_hbm,
    second_hbm,
    shift_hbm,
    cos_hbm,
    out_ref,
    xv,
    halo,
    tapv,
    firstv,
    turnv,
    secondv,
    shiftv,
    cosv,
    y,
    u,
    vhi,
    vlo,
    white,
    mine,
    got,
    cross0,
    cross12,
    held,
    part0,
    part12,
    recv0,
    recv12,
    load_sem,
    come,
    halo_sem,
    white_send,
    white_recv,
    p0_send,
    p0_recv,
    p12_send,
    p12_recv,
):
    b = lax.axis_index("sta")
    j = lax.axis_index("tm")
    lanes = 2 * HALF_LAGS // n_tm
    group = n_tm // 2

    barrier = pltpu.get_barrier_semaphore()
    neighbours = [(b, lax.rem(j + 1, n_tm)), (b, lax.rem(j + n_tm - 1, n_tm))]
    peers = list(neighbours)
    odd = lax.rem(b, 2)
    ahead = (lax.rem(b + 2, n_sta), j)
    behind = (lax.rem(b + n_sta - 2, n_sta), j)
    sibling = (b + 1 - 2 * odd, j)
    across = (lax.rem(b + n_sta - 3 + 6 * odd, n_sta), j)
    third = (lax.rem(b + n_sta - 3 + 2 * odd, n_sta), j)
    peers += [ahead, behind, sibling, across]
    for peer in peers:
        pl.semaphore_signal(barrier, inc=1, device_id=peer, device_id_type=MESH)

    def pass_on(step):
        for neighbour in neighbours:
            pl.semaphore_signal(
                come.at[step], inc=1, device_id=neighbour, device_id_type=MESH
            )

    loads = []
    for idx, (src, dst) in enumerate(
        [
            (x_hbm, xv),
            (tap_hbm, tapv),
            (first_hbm, firstv),
            (turn_hbm, turnv),
            (second_hbm, secondv),
            (shift_hbm, shiftv),
            (cos_hbm, cosv),
        ]
    ):
        loads.append(pltpu.make_async_copy(src, dst, load_sem.at[idx]))
    for copy in loads[:-1]:
        copy.start()

    loads[0].wait()
    pl.semaphore_wait(barrier, len(peers))
    halo_copies = []
    for part in range(4):
        rows = pl.ds(8 * part, 8)
        copy = pltpu.make_async_remote_copy(
            src_ref=xv.at[rows],
            dst_ref=halo.at[rows],
            send_sem=halo_sem.at[0, part],
            recv_sem=halo_sem.at[1, part],
            device_id=(b, lax.rem(j + n_tm - 1, n_tm)),
            device_id_type=MESH,
        )
        copy.start()
        halo_copies.append(copy)
    pass_on(0)

    station = lax.broadcasted_iota(jnp.int32, (ST, 128), 0)
    live = (station < counts[0]).astype(F32)

    lane = lax.broadcasted_iota(jnp.int32, (ST, 128), 1)
    opposite = jnp.where(lane < 64, (64 - lane) & 63, 191 - lane)

    def by_lane(value, index):
        return jnp.take_along_axis(value, index, axis=1, mode="promise_in_bounds")

    def first_step(frames):
        total = jnp.sum(jnp.sum(frames, axis=0), axis=1, keepdims=True)
        frames = (frames - (total * (1.0 / LENGTH))[None]) * tapv[...]
        frames = frames.reshape(64 * ST, 128)
        high = frames.astype(BF16)
        y[:, 0:128] = high
        y[:, 128:256] = (frames - high.astype(F32)).astype(BF16)
        both = jnp.dot(firstv[0], y[...], preferred_element_type=F32)
        u[...] = (
            both[:, 0:128]
            + both[:, 128:256]
            + jnp.dot(firstv[1], y[:, 0:128], preferred_element_type=F32)
        ).reshape(2 * LIVE_ROWS, ST, 128)

    def turned(row):
        re0, im0 = u[row], u[LIVE_ROWS + row]
        re1, im1 = (u[32], u[LIVE_ROWS + 32]) if row == 0 else (re0, im0)
        c0, s0, c1, s1 = turnv[0, row], turnv[1, row], turnv[2, row], turnv[3, row]
        return (
            re0 * c0 + im0 * s0,
            im0 * c0 - re0 * s0,
            re1 * c1 - im1 * s1,
            -(im1 * c1 + re1 * s1),
        )

    def mirrored_bins(value):
        first = jnp.where(lane == 0, 0.0, by_lane(value[0], opposite))
        return jnp.concatenate([first[None], pltpu.roll(value[1:], 64, 2)])

    def second_step(w):
        for i in range(16):
            pair = zip(turned(2 * i), turned(2 * i + 1))
            for block, (upper, lower) in enumerate(pair):
                v = jnp.concatenate([upper, lower], axis=0)
                high = v.astype(BF16)
                vhi[16 * i : 16 * i + 16, 128 * block : 128 * block + 128] = high
                vlo[16 * i : 16 * i + 16, 128 * block : 128 * block + 128] = (
                    v - high.astype(F32)
                ).astype(BF16)
        spec = (
            jnp.dot(vhi[...], secondv[0], preferred_element_type=F32)
            + jnp.dot(vlo[...], secondv[0], preferred_element_type=F32)
            + jnp.dot(vhi[...], secondv[1], preferred_element_type=F32)
        )
        re = spec[:, 0:128].reshape(32, ST, 128)
        im = spec[:, 128:256].reshape(32, ST, 128)
        energy = jnp.sum(re * re + im * im, axis=0)
        energy = (energy + by_lane(energy, 127 - lane)) * (1.0 / BAND)
        scale = live / jnp.sqrt(energy + 1e-06)
        re = (re * scale[None]).reshape(2, 128, 128).astype(BF16)
        im = (im * scale[None]).reshape(2, 128, 128).astype(BF16)
        for part in range(2):
            white[w, part, 0] = re[part]
            white[w, part, 1] = im[part]

    def shifted(w):
        re = white[w, :, 0].astype(F32).reshape(32, ST, 128)
        im = white[w, :, 1].astype(F32).reshape(32, ST, 128)
        left = (re * shiftv[0] + im * shiftv[1], im * shiftv[0] - re * shiftv[1])
        for c in range(2):
            mine[w, c] = left[c]
            mine[w, 2 + c] = mirrored_bins(left[c])

    def start_white(w, part, place, source, to):
        copy = pltpu.make_async_remote_copy(
            src_ref=source,
            dst_ref=got.at[w, part, place],
            send_sem=white_send.at[w, part, place],
            recv_sem=white_recv.at[w, part, place],
            device_id=to,
            device_id_type=MESH,
        )
        copy.start()
        return copy

    def send_near(w):
        return [[start_white(w, part, 0, white.at[w, part], behind)] for part in range(2)]

    def send_far(w, copies):
        for part in range(2):
            copies[part].append(start_white(w, part, 1, white.at[w, part], third))

    def hand_on(w, part, copies):
        copies[part][0].wait()
        copies[part].append(start_white(w, part, 2, got.at[w, part, 0], sibling))

    for copy in loads[1:-1]:
        copy.wait()
    first_step(xv[...])
    second_step(0)
    loads[-1].start()
    sent0 = send_near(0)
    send_far(0, sent0)
    pl.semaphore_wait(come.at[0], 2)
    pass_on(1)
    shifted(0)
    for copy in halo_copies:
        copy.wait()
    inside = (j < n_tm - 1).astype(F32)
    first_step(jnp.concatenate([xv[32:64], halo[...] * inside], axis=0))
    second_step(1)
    sent1 = send_near(1)
    pl.semaphore_wait(come.at[1], 2)
    pass_on(2)
    shifted(1)

    def cross_pair(others, cross, slots, windows, part, i):
        right = others(part, slice(16 * i, 16 * i + 16), windows)
        for half in range(2):
            row = 16 * part + 2 * i + half
            at = slice(128 * row, 128 * row + 128)
            own = slice(8 * half, 8 * half + 8)
            terms = []
            for slot in range(slots):
                terms.append([])
                for pair in right[slot]:
                    values = [value[own] for value in pair]
                    if row == 0:
                        values += [by_lane(value, opposite) for value in values]
                    else:
                        values += [pltpu.roll(value, 64, 1) for value in values]
                    terms[slot].append(values)
            for s in range(0, ST, 2):
                kept = [[], []]
                for t in (s, s + 1):
                    left = [
                        [
                            jnp.broadcast_to(mine[w, c, row, t : t + 1, :], (ST, 128))
                            for c in range(4)
                        ]
                        for w in windows
                    ]
                    for slot in range(slots):
                        re, im = None, None
                        for mine_values, values in zip(left, terms[slot]):
                            a_re, a_im, back_re, back_im = mine_values
                            o_re, o_im, other_re, other_im = values
                            new_re = a_re * o_re + a_im * o_im
                            new_im = back_im * other_re - back_re * other_im
                            re = new_re if re is None else re + new_re
                            im = new_im if im is None else im + new_im
                        kept[0].append(re - im)
                        kept[1].append(re + im)
                for slot in range(slots):
                    for sign in range(2):
                        at_rows = pl.ds((sign * slots + slot) * PAIRS + s * ST, 16)
                        cross[at_rows, at] = jnp.concatenate(
                            [kept[sign][slot], kept[sign][slots + slot]], axis=0
                        ).astype(BF16)

    def cross_terms(others, cross, slots, windows, part):
        for i in range(8):
            cross_pair(others, cross, slots, windows, part, i)

    def lag_sums(cross, half):
        return jnp.dot(cross[...], cosv[half], preferred_element_type=F32)

    def keep_part(sums, half, part):
        rows = sums.shape[0] // 2
        even = (lax.broadcasted_iota(jnp.int32, (rows, 256), 1) & 1) == 0
        minus, plus = sums[:rows], sums[rows:]
        later = jnp.where(even, minus, plus).astype(BF16)
        earlier = jnp.where(even, plus, minus).astype(BF16)
        for e in range(n_tm // 4):
            at = slice(lanes * e, lanes * e + lanes)
            block = half * (n_tm // 4) + e
            part[group + block] = later[:, at]
            part[group - 1 - block] = earlier[:, at]

    def send_part(part, recv, send_sem, recv_sem):
        copies = []
        for d in sorted(range(1, n_tm), key=lambda d: -min(d, n_tm - d)):
            to = lax.rem(j + d, n_tm)
            copy = pltpu.make_async_remote_copy(
                src_ref=part.at[to],
                dst_ref=recv.at[d - 1],
                send_sem=send_sem.at[d - 1],
                recv_sem=recv_sem.at[d - 1],
                device_id=(b, to),
                device_id_type=MESH,
            )
            copy.start()
            copies.append((d, copy))
        return copies

    def own_rows(part, rows, windows):
        return [[[white[w, part, c, rows, :].astype(F32) for c in range(2)] for w in windows]]

    cross_terms(own_rows, cross0, 1, (0, 1), 0)
    send_far(1, sent1)
    hand_on(0, 0, sent0)
    hand_on(0, 1, sent0)
    cross_terms(own_rows, cross0, 1, (0, 1), 1)
    loads[-1].wait()
    pl.semaphore_wait(come.at[2], 2)
    for half in range(2):
        keep_part(lag_sums(cross0, half), half, part0)
    terms0 = send_part(part0, recv0, p0_send, p0_recv)

    offsets = (2, 1 + 2 * odd, 3 - 2 * odd)
    takes = [
        [(partners[slot] == b + offset).astype(F32) for offset in offsets]
        for slot in range(1, SLOTS)
    ]

    def chosen(part, rows, windows):
        slots = [[] for _ in takes]
        for w in windows:
            pairs = [[] for _ in takes]
            for c in range(2):
                values = [got[w, part, d, c, rows, :].astype(F32) for d in range(REACH)]
                for pair, take in zip(pairs, takes):
                    pair.append(values[0] * take[0] + values[1] * take[1] + values[2] * take[2])
            for slot, pair in zip(slots, pairs):
                slot.append(pair)
        return slots

    for part in range(2):
        for copy in sent0[part][1:]:
            copy.wait()
        cross_terms(chosen, cross12, SLOTS - 1, (0,), part)
    hand_on(1, 0, sent1)
    hand_on(1, 1, sent1)
    for half in range(2):
        held[half] = lag_sums(cross12, half)
    for part in range(2):
        for copy in sent1[part][1:]:
            copy.wait()
        cross_terms(chosen, cross12, SLOTS - 1, (1,), part)
    for half in range(2):
        keep_part(held[half] + lag_sums(cross12, half), half, part12)
    terms12 = send_part(part12, recv12, p12_send, p12_recv)

    at = lax.broadcasted_iota(jnp.int32, (ST, lanes), 1)
    at = jnp.where(j >= group, at, lanes - 1 - at)

    def finish(part, recv, copies):
        total = part[j].astype(F32)
        for d, copy in reversed(copies):
            copy.wait()
            total = total + recv[d - 1].astype(F32)
        blocks = [by_lane(total[r : r + ST], at) for r in range(0, total.shape[0], ST)]
        return jnp.concatenate(blocks, axis=0)

    own = finish(part0, recv0, terms0)
    pair = lax.broadcasted_iota(jnp.int32, (PAIRS, lanes), 0)
    own = jnp.where((pair >> 3) == (pair & 7), 0.0, own)
    out_ref[0:PAIRS, :] = own
    out_ref[PAIRS : SLOTS * PAIRS, :] = finish(part12, recv12, terms12)


def shards(n_sta, n_tm, traces, station_counts, partners):
    x = traces.reshape(ST, 64, 128).transpose(1, 0, 2)
    consts = [jnp.asarray(table) for table in tables()]
    lanes = 2 * HALF_LAGS // n_tm
    anywhere = pl.BlockSpec(memory_space=pl.ANY)
    scalars = pl.BlockSpec(memory_space=pltpu.SMEM)
    dma = pltpu.SemaphoreType.DMA
    series = pl.pallas_call(
        functools.partial(kernel, n_sta, n_tm),
        out_shape=jax.ShapeDtypeStruct((SLOTS * PAIRS, lanes), F32),
        in_specs=[anywhere, scalars, scalars] + [anywhere] * len(consts),
        out_specs=pl.BlockSpec(memory_space=pltpu.VMEM),
        scratch_shapes=[
            pltpu.VMEM((64, ST, 128), F32),
            pltpu.VMEM((32, ST, 128), F32),
            *[pltpu.VMEM(table.shape, table.dtype) for table in consts],
            pltpu.VMEM((64 * ST, 256), BF16),
            pltpu.VMEM((2 * LIVE_ROWS, ST, 128), F32),
            pltpu.VMEM((256, 512), BF16),
            pltpu.VMEM((256, 512), BF16),
            pltpu.VMEM((2, 2, 2, 128, 128), BF16),
            pltpu.VMEM((2, 4, 32, ST, 128), F32),
            pltpu.VMEM((2, 2, REACH, 2, 128, 128), BF16),
            pltpu.VMEM((2 * PAIRS, FREQ), BF16),
            pltpu.VMEM((4 * PAIRS, FREQ), BF16),
            pltpu.VMEM((2, 4 * PAIRS, 256), F32),
            pltpu.VMEM((n_tm, PAIRS, lanes), BF16),
            pltpu.VMEM((n_tm, 2 * PAIRS, lanes), BF16),
            pltpu.VMEM((n_tm - 1, PAIRS, lanes), BF16),
            pltpu.VMEM((n_tm - 1, 2 * PAIRS, lanes), BF16),
            dma((7,)),
            pltpu.SemaphoreType.REGULAR((n_tm // 2 - 1,)),
            dma((2, 4)),
            dma((2, 2, REACH)),
            dma((2, 2, REACH)),
            dma((n_tm - 1,)),
            dma((n_tm - 1,)),
            dma((n_tm - 1,)),
            dma((n_tm - 1,)),
        ],
        compiler_params=pltpu.CompilerParams(
            collective_id=0, has_side_effects=True, vmem_limit_bytes=VMEM_LIMIT
        ),
    )(x, station_counts, partners.reshape(SLOTS), *consts)
    norm = 1.0 / math.sqrt(2.0 * LENGTH * n_tm)
    return (series * norm).reshape(1, SLOTS, ST, ST, lanes)


def solution(mesh):
    placed = (P("sta", "tm"), P("sta"), P("sta", None))
    return jax.shard_map(
        functools.partial(shards, mesh.shape["sta"], mesh.shape["tm"]),
        mesh=mesh,
        in_specs=placed,
        out_specs=P("sta", None, None, None, "tm"),
        check_vma=False,
    )
```

```python
import functools
import math

import jax
import jax.numpy as jnp
import ml_dtypes
import numpy as np
from jax import lax
from jax.experimental import pallas as pl
from jax.experimental.pallas import tpu as pltpu
from jax.sharding import PartitionSpec as P

MESH = pl.DeviceIdType.MESH
F32 = jnp.float32
BF16 = jnp.bfloat16

ST = 8
FREQ = 4096
LENGTH = 2 * FREQ
BAND = 64
HALF_LAGS = 512
SLOTS = 3
REACH = 3
PAIRS = ST * ST
VMEM_LIMIT = 55100 * 2**10
LIVE_ROWS = 33


def split(table):
    high = table.astype(ml_dtypes.bfloat16)
    low = (table - high.astype(np.float64)).astype(ml_dtypes.bfloat16)
    return np.stack([high, low])


def tables():
    m = np.arange(64)
    q = np.arange(128)
    taper = 0.5 - 0.5 * np.cos(np.arange(LENGTH) * (2.0 * math.pi / LENGTH))
    taper = np.repeat(taper.astype(np.float32).reshape(64, 1, 128), ST, axis=1)
    angle = 2.0 * math.pi * (np.outer(np.arange(LIVE_ROWS), m) % 64) / 64
    first = split(np.kron(np.concatenate([np.cos(angle), -np.sin(angle)]), np.eye(ST)))
    ids = np.arange(32)
    mirrored = np.where(ids == 0, 32, 64 - ids)
    near = 2.0 * math.pi * np.outer(ids, q) / LENGTH
    far = 2.0 * math.pi * np.outer(mirrored, q) / LENGTH
    turn = np.stack([np.cos(near), np.sin(near), np.cos(far), np.sin(far)])
    turn = np.repeat(turn.astype(np.float32)[:, :, None, :], ST, axis=2)
    k = np.arange(BAND)
    angle = 2.0 * math.pi * (np.outer(q, k) % 128) / 128
    cos, sin, none = np.cos(angle), np.sin(angle), np.zeros((128, BAND))
    back_cos, back_sin = cos[:, ::-1], sin[:, ::-1]
    second = np.concatenate(
        [
            np.concatenate([cos, none, -sin, none], axis=1),
            np.concatenate([sin, none, cos, none], axis=1),
            np.concatenate([none, back_cos, none, -back_sin], axis=1),
            np.concatenate([none, back_sin, none, back_cos], axis=1),
        ]
    )
    second = split(second)
    bins = np.concatenate(
        [64 * k[None, :] + ids[:, None], 64 * (63 - k)[None, :] + mirrored[:, None]], axis=1
    )
    angle = math.pi * bins / LENGTH
    shift = np.stack([np.cos(angle), np.sin(angle)]).astype(np.float32)
    shift = np.repeat(shift[:, :, None, :], ST, axis=2)
    order = bins.reshape(-1)
    steps = np.outer(order, 2 * np.arange(HALF_LAGS) + 1) % (2 * LENGTH)
    weight = np.where(order == 0, 1.0, 2.0)
    lag_cos = weight[:, None] * np.cos(math.pi * steps / LENGTH)
    lag_cos = lag_cos.reshape(FREQ, 2, 256).transpose(1, 0, 2).astype(ml_dtypes.bfloat16)
    return taper, first, turn, second, shift, lag_cos


def kernel(
    n_sta,
    n_tm,
    x_hbm,
    counts,
    partners,
    tap_hbm,
    first_hbm,
    turn_hbm,
    second_hbm,
    shift_hbm,
    cos_hbm,
    out_ref,
    xv,
    halo,
    tapv,
    firstv,
    turnv,
    secondv,
    shiftv,
    cosv,
    y,
    u,
    vhi,
    vlo,
    white,
    mine,
    got,
    cross0,
    cross12,
    held,
    part0,
    part12,
    recv0,
    recv12,
    load_sem,
    come,
    halo_sem,
    white_send,
    white_recv,
    p0_send,
    p0_recv,
    p12_send,
    p12_recv,
):
    b = lax.axis_index("sta")
    j = lax.axis_index("tm")
    lanes = 2 * HALF_LAGS // n_tm
    group = n_tm // 2

    barrier = pltpu.get_barrier_semaphore()
    neighbours = [(b, lax.rem(j + 1, n_tm)), (b, lax.rem(j + n_tm - 1, n_tm))]
    odd = lax.rem(b, 2)
    ahead = (lax.rem(b + 2, n_sta), j)
    behind = (lax.rem(b + n_sta - 2, n_sta), j)
    sibling = (b + 1 - 2 * odd, j)
    across = (lax.rem(b + n_sta - 3 + 6 * odd, n_sta), j)
    third = (lax.rem(b + n_sta - 3 + 2 * odd, n_sta), j)
    has_ahead, has_behind = b < n_sta - 2, b >= 2
    sends = [has_behind, (odd == 1) | (b >= 4), has_ahead]
    receives = [has_ahead, (odd == 0) | (b < n_sta - 3), has_ahead]
    has_across = ((odd == 1) & (b < n_sta - 3)) | ((odd == 0) & (b >= 4))
    for peer in neighbours + [sibling]:
        pl.semaphore_signal(barrier, inc=1, device_id=peer, device_id_type=MESH)
    for there, peer in ((has_ahead, ahead), (has_behind, behind), (has_across, across)):
        pl.when(there)(
            functools.partial(
                pl.semaphore_signal, barrier, inc=1, device_id=peer, device_id_type=MESH
            )
        )
    arrivals = 3
    for there in (has_ahead, has_behind, has_across):
        arrivals = arrivals + there.astype(jnp.int32)

    for place in range(REACH):

        @pl.when(jnp.logical_not(receives[place]))
        def _():
            for w in range(2):
                for part in range(2):
                    got[w, part, place] = jnp.zeros((2, 128, 128), BF16)

    def pass_on(step):
        for neighbour in neighbours:
            pl.semaphore_signal(
                come.at[step], inc=1, device_id=neighbour, device_id_type=MESH
            )

    loads = []
    for idx, (src, dst) in enumerate(
        [
            (x_hbm, xv),
            (tap_hbm, tapv),
            (first_hbm, firstv),
            (turn_hbm, turnv),
            (second_hbm, secondv),
            (shift_hbm, shiftv),
            (cos_hbm, cosv),
        ]
    ):
        loads.append(pltpu.make_async_copy(src, dst, load_sem.at[idx]))
    for copy in loads[:-1]:
        copy.start()

    loads[0].wait()
    pl.semaphore_wait(barrier, arrivals)
    halo_copies = []
    for part in range(4):
        rows = pl.ds(8 * part, 8)
        copy = pltpu.make_async_remote_copy(
            src_ref=xv.at[rows],
            dst_ref=halo.at[rows],
            send_sem=halo_sem.at[0, part],
            recv_sem=halo_sem.at[1, part],
            device_id=(b, lax.rem(j + n_tm - 1, n_tm)),
            device_id_type=MESH,
        )
        copy.start()
        halo_copies.append(copy)
    pass_on(0)

    station = lax.broadcasted_iota(jnp.int32, (ST, 128), 0)
    live = (station < counts[0]).astype(F32)

    lane = lax.broadcasted_iota(jnp.int32, (ST, 128), 1)
    opposite = jnp.where(lane < 64, (64 - lane) & 63, 191 - lane)

    def by_lane(value, index):
        return jnp.take_along_axis(value, index, axis=1, mode="promise_in_bounds")

    def first_step(frames):
        total = jnp.sum(jnp.sum(frames, axis=0), axis=1, keepdims=True)
        frames = (frames - (total * (1.0 / LENGTH))[None]) * tapv[...]
        frames = frames.reshape(64 * ST, 128)
        high = frames.astype(BF16)
        y[:, 0:128] = high
        y[:, 128:256] = (frames - high.astype(F32)).astype(BF16)
        both = jnp.dot(firstv[0], y[...], preferred_element_type=F32)
        u[...] = (
            both[:, 0:128]
            + both[:, 128:256]
            + jnp.dot(firstv[1], y[:, 0:128], preferred_element_type=F32)
        ).reshape(2 * LIVE_ROWS, ST, 128)

    def turned(row):
        re0, im0 = u[row], u[LIVE_ROWS + row]
        re1, im1 = (u[32], u[LIVE_ROWS + 32]) if row == 0 else (re0, im0)
        c0, s0, c1, s1 = turnv[0, row], turnv[1, row], turnv[2, row], turnv[3, row]
        return (
            re0 * c0 + im0 * s0,
            im0 * c0 - re0 * s0,
            re1 * c1 - im1 * s1,
            -(im1 * c1 + re1 * s1),
        )

    def mirrored_bins(value):
        first = jnp.where(lane == 0, 0.0, by_lane(value[0], opposite))
        return jnp.concatenate([first[None], pltpu.roll(value[1:], 64, 2)])

    def second_step(w):
        for i in range(16):
            pair = zip(turned(2 * i), turned(2 * i + 1))
            for block, (upper, lower) in enumerate(pair):
                v = jnp.concatenate([upper, lower], axis=0)
                high = v.astype(BF16)
                vhi[16 * i : 16 * i + 16, 128 * block : 128 * block + 128] = high
                vlo[16 * i : 16 * i + 16, 128 * block : 128 * block + 128] = (
                    v - high.astype(F32)
                ).astype(BF16)
        spec = (
            jnp.dot(vhi[...], secondv[0], preferred_element_type=F32)
            + jnp.dot(vlo[...], secondv[0], preferred_element_type=F32)
            + jnp.dot(vhi[...], secondv[1], preferred_element_type=F32)
        )
        re = spec[:, 0:128].reshape(32, ST, 128)
        im = spec[:, 128:256].reshape(32, ST, 128)
        energy = jnp.sum(re * re + im * im, axis=0)
        energy = (energy + by_lane(energy, 127 - lane)) * (1.0 / BAND)
        scale = live / jnp.sqrt(energy + 1e-06)
        re = (re * scale[None]).reshape(2, 128, 128).astype(BF16)
        im = (im * scale[None]).reshape(2, 128, 128).astype(BF16)
        for part in range(2):
            white[w, part, 0] = re[part]
            white[w, part, 1] = im[part]

    def shifted(w):
        re = white[w, :, 0].astype(F32).reshape(32, ST, 128)
        im = white[w, :, 1].astype(F32).reshape(32, ST, 128)
        left = (re * shiftv[0] + im * shiftv[1], im * shiftv[0] - re * shiftv[1])
        for c in range(2):
            mine[w, c] = left[c]
            mine[w, 2 + c] = mirrored_bins(left[c])

    def start_white(w, part, place, source, to):
        copy = pltpu.make_async_remote_copy(
            src_ref=source,
            dst_ref=got.at[w, part, place],
            send_sem=white_send.at[w, part, place],
            recv_sem=white_recv.at[w, part, place],
            device_id=to,
            device_id_type=MESH,
        )
        pl.when(sends[place])(copy.start)
        return copy

    def send_near(w):
        return [[start_white(w, part, 0, white.at[w, part], behind)] for part in range(2)]

    def send_far(w, copies):
        for part in range(2):
            copies[part].append(start_white(w, part, 1, white.at[w, part], third))

    def hand_on(w, part, copies):
        pl.when(receives[0])(copies[part][0].wait_recv)
        copies[part].append(start_white(w, part, 2, got.at[w, part, 0], sibling))

    def arrive(copies):
        for place in (1, 2):
            pl.when(receives[place])(copies[place].wait_recv)

    for copy in loads[1:-1]:
        copy.wait()
    first_step(xv[...])
    second_step(0)
    loads[-1].start()
    sent0 = send_near(0)
    send_far(0, sent0)
    pl.semaphore_wait(come.at[0], 2)
    pass_on(1)
    shifted(0)
    for copy in halo_copies:
        copy.wait()
    inside = (j < n_tm - 1).astype(F32)
    first_step(jnp.concatenate([xv[32:64], halo[...] * inside], axis=0))
    second_step(1)
    sent1 = send_near(1)
    pl.semaphore_wait(come.at[1], 2)
    pass_on(2)
    shifted(1)

    def cross_pair(others, cross, slots, windows, part, i):
        right = others(part, slice(16 * i, 16 * i + 16), windows)
        for half in range(2):
            row = 16 * part + 2 * i + half
            at = slice(128 * row, 128 * row + 128)
            own = slice(8 * half, 8 * half + 8)
            terms = []
            for slot in range(slots):
                terms.append([])
                for pair in right[slot]:
                    values = [value[own] for value in pair]
                    if row == 0:
                        values += [by_lane(value, opposite) for value in values]
                    else:
                        values += [pltpu.roll(value, 64, 1) for value in values]
                    terms[slot].append(values)
            for s in range(0, ST, 2):
                kept = [[], []]
                for t in (s, s + 1):
                    left = [
                        [
                            jnp.broadcast_to(mine[w, c, row, t : t + 1, :], (ST, 128))
                            for c in range(4)
                        ]
                        for w in windows
                    ]
                    for slot in range(slots):
                        re, im = None, None
                        for mine_values, values in zip(left, terms[slot]):
                            a_re, a_im, back_re, back_im = mine_values
                            o_re, o_im, other_re, other_im = values
                            new_re = a_re * o_re + a_im * o_im
                            new_im = back_im * other_re - back_re * other_im
                            re = new_re if re is None else re + new_re
                            im = new_im if im is None else im + new_im
                        kept[0].append(re - im)
                        kept[1].append(re + im)
                for slot in range(slots):
                    for sign in range(2):
                        at_rows = pl.ds((sign * slots + slot) * PAIRS + s * ST, 16)
                        cross[at_rows, at] = jnp.concatenate(
                            [kept[sign][slot], kept[sign][slots + slot]], axis=0
                        ).astype(BF16)

    def cross_terms(others, cross, slots, windows, part):
        for i in range(8):
            cross_pair(others, cross, slots, windows, part, i)

    def lag_sums(cross, half):
        return jnp.dot(cross[...], cosv[half], preferred_element_type=F32)

    def keep_part(sums, half, part):
        rows = sums.shape[0] // 2
        even = (lax.broadcasted_iota(jnp.int32, (rows, 256), 1) & 1) == 0
        minus, plus = sums[:rows], sums[rows:]
        later = jnp.where(even, minus, plus).astype(BF16)
        earlier = jnp.where(even, plus, minus).astype(BF16)
        for e in range(n_tm // 4):
            at = slice(lanes * e, lanes * e + lanes)
            block = half * (n_tm // 4) + e
            part[group + block] = later[:, at]
            part[group - 1 - block] = earlier[:, at]

    def send_part(part, recv, send_sem, recv_sem):
        copies = []
        for d in sorted(range(1, n_tm), key=lambda d: -min(d, n_tm - d)):
            to = lax.rem(j + d, n_tm)
            copy = pltpu.make_async_remote_copy(
                src_ref=part.at[to],
                dst_ref=recv.at[d - 1],
                send_sem=send_sem.at[d - 1],
                recv_sem=recv_sem.at[d - 1],
                device_id=(b, to),
                device_id_type=MESH,
            )
            copy.start()
            copies.append((d, copy))
        return copies

    def own_rows(part, rows, windows):
        return [[[white[w, part, c, rows, :].astype(F32) for c in range(2)] for w in windows]]

    cross_terms(own_rows, cross0, 1, (0, 1), 0)
    send_far(1, sent1)
    hand_on(0, 0, sent0)
    hand_on(0, 1, sent0)
    cross_terms(own_rows, cross0, 1, (0, 1), 1)
    loads[-1].wait()
    pl.semaphore_wait(come.at[2], 2)
    for half in range(2):
        keep_part(lag_sums(cross0, half), half, part0)
    terms0 = send_part(part0, recv0, p0_send, p0_recv)

    offsets = (2, 1 + 2 * odd, 3 - 2 * odd)
    takes = [
        [(partners[slot] == b + offset).astype(F32) for offset in offsets]
        for slot in range(1, SLOTS)
    ]

    def chosen(part, rows, windows):
        slots = [[] for _ in takes]
        for w in windows:
            pairs = [[] for _ in takes]
            for c in range(2):
                values = [got[w, part, d, c, rows, :].astype(F32) for d in range(REACH)]
                for pair, take in zip(pairs, takes):
                    pair.append(values[0] * take[0] + values[1] * take[1] + values[2] * take[2])
            for slot, pair in zip(slots, pairs):
                slot.append(pair)
        return slots

    for part in range(2):
        arrive(sent0[part])
        cross_terms(chosen, cross12, SLOTS - 1, (0,), part)
    hand_on(1, 0, sent1)
    hand_on(1, 1, sent1)
    for half in range(2):
        held[half] = lag_sums(cross12, half)
    for part in range(2):
        arrive(sent1[part])
        cross_terms(chosen, cross12, SLOTS - 1, (1,), part)
    for half in range(2):
        keep_part(held[half] + lag_sums(cross12, half), half, part12)
    terms12 = send_part(part12, recv12, p12_send, p12_recv)

    at = lax.broadcasted_iota(jnp.int32, (ST, lanes), 1)
    at = jnp.where(j >= group, at, lanes - 1 - at)

    def finish(part, recv, copies):
        total = part[j].astype(F32)
        for d, copy in reversed(copies):
            copy.wait()
            total = total + recv[d - 1].astype(F32)
        blocks = [by_lane(total[r : r + ST], at) for r in range(0, total.shape[0], ST)]
        return jnp.concatenate(blocks, axis=0)

    for copies in sent0 + sent1:
        for place, copy in enumerate(copies):
            pl.when(sends[place])(copy.wait_send)
    own = finish(part0, recv0, terms0)
    pair = lax.broadcasted_iota(jnp.int32, (PAIRS, lanes), 0)
    own = jnp.where((pair >> 3) == (pair & 7), 0.0, own)
    out_ref[0:PAIRS, :] = own
    out_ref[PAIRS : SLOTS * PAIRS, :] = finish(part12, recv12, terms12)


def shards(n_sta, n_tm, traces, station_counts, partners):
    x = traces.reshape(ST, 64, 128).transpose(1, 0, 2)
    consts = [jnp.asarray(table) for table in tables()]
    lanes = 2 * HALF_LAGS // n_tm
    anywhere = pl.BlockSpec(memory_space=pl.ANY)
    scalars = pl.BlockSpec(memory_space=pltpu.SMEM)
    dma = pltpu.SemaphoreType.DMA
    series = pl.pallas_call(
        functools.partial(kernel, n_sta, n_tm),
        out_shape=jax.ShapeDtypeStruct((SLOTS * PAIRS, lanes), F32),
        in_specs=[anywhere, scalars, scalars] + [anywhere] * len(consts),
        out_specs=pl.BlockSpec(memory_space=pltpu.VMEM),
        scratch_shapes=[
            pltpu.VMEM((64, ST, 128), F32),
            pltpu.VMEM((32, ST, 128), F32),
            *[pltpu.VMEM(table.shape, table.dtype) for table in consts],
            pltpu.VMEM((64 * ST, 256), BF16),
            pltpu.VMEM((2 * LIVE_ROWS, ST, 128), F32),
            pltpu.VMEM((256, 512), BF16),
            pltpu.VMEM((256, 512), BF16),
            pltpu.VMEM((2, 2, 2, 128, 128), BF16),
            pltpu.VMEM((2, 4, 32, ST, 128), F32),
            pltpu.VMEM((2, 2, REACH, 2, 128, 128), BF16),
            pltpu.VMEM((2 * PAIRS, FREQ), BF16),
            pltpu.VMEM((4 * PAIRS, FREQ), BF16),
            pltpu.VMEM((2, 4 * PAIRS, 256), F32),
            pltpu.VMEM((n_tm, PAIRS, lanes), BF16),
            pltpu.VMEM((n_tm, 2 * PAIRS, lanes), BF16),
            pltpu.VMEM((n_tm - 1, PAIRS, lanes), BF16),
            pltpu.VMEM((n_tm - 1, 2 * PAIRS, lanes), BF16),
            dma((7,)),
            pltpu.SemaphoreType.REGULAR((n_tm // 2 - 1,)),
            dma((2, 4)),
            dma((2, 2, REACH)),
            dma((2, 2, REACH)),
            dma((n_tm - 1,)),
            dma((n_tm - 1,)),
            dma((n_tm - 1,)),
            dma((n_tm - 1,)),
        ],
        compiler_params=pltpu.CompilerParams(
            collective_id=0, has_side_effects=True, vmem_limit_bytes=VMEM_LIMIT
        ),
    )(x, station_counts, partners.reshape(SLOTS), *consts)
    norm = 1.0 / math.sqrt(2.0 * LENGTH * n_tm)
    return (series * norm).reshape(1, SLOTS, ST, ST, lanes)


def solution(mesh):
    placed = (P("sta", "tm"), P("sta"), P("sta", None))
    return jax.shard_map(
        functools.partial(shards, mesh.shape["sta"], mesh.shape["tm"]),
        mesh=mesh,
        in_specs=placed,
        out_specs=P("sta", None, None, None, "tm"),
        check_vma=False,
    )
```

```python
import functools
import math

import jax
import jax.numpy as jnp
import ml_dtypes
import numpy as np
from jax import lax
from jax.experimental import pallas as pl
from jax.experimental.pallas import tpu as pltpu
from jax.sharding import PartitionSpec as P

MESH = pl.DeviceIdType.MESH
F32 = jnp.float32
BF16 = jnp.bfloat16

ST = 8
FREQ = 4096
LENGTH = 2 * FREQ
BAND = 64
HALF_LAGS = 512
SLOTS = 3
REACH = 3
PAIRS = ST * ST
VMEM_LIMIT = 55100 * 2**10
LIVE_ROWS = 33


def split(table):
    high = table.astype(ml_dtypes.bfloat16)
    low = (table - high.astype(np.float64)).astype(ml_dtypes.bfloat16)
    return np.stack([high, low])


def tables():
    m = np.arange(64)
    q = np.arange(128)
    taper = 0.5 - 0.5 * np.cos(np.arange(LENGTH) * (2.0 * math.pi / LENGTH))
    taper = np.repeat(taper.astype(np.float32).reshape(64, 1, 128), ST, axis=1)
    angle = 2.0 * math.pi * (np.outer(np.arange(LIVE_ROWS), m) % 64) / 64
    first = split(np.kron(np.concatenate([np.cos(angle), -np.sin(angle)]), np.eye(ST)))
    ids = np.arange(32)
    mirrored = np.where(ids == 0, 32, 64 - ids)
    near = 2.0 * math.pi * np.outer(ids, q) / LENGTH
    far = 2.0 * math.pi * np.outer(mirrored, q) / LENGTH
    turn = np.stack([np.cos(near), np.sin(near), np.cos(far), np.sin(far)])
    turn = np.repeat(turn.astype(np.float32)[:, :, None, :], ST, axis=2)
    k = np.arange(BAND)
    angle = 2.0 * math.pi * (np.outer(q, k) % 128) / 128
    cos, sin, none = np.cos(angle), np.sin(angle), np.zeros((128, BAND))
    back_cos, back_sin = cos[:, ::-1], sin[:, ::-1]
    second = np.concatenate(
        [
            np.concatenate([cos, none, -sin, none], axis=1),
            np.concatenate([sin, none, cos, none], axis=1),
            np.concatenate([none, back_cos, none, -back_sin], axis=1),
            np.concatenate([none, back_sin, none, back_cos], axis=1),
        ]
    )
    second = split(second)
    bins = np.concatenate(
        [64 * k[None, :] + ids[:, None], 64 * (63 - k)[None, :] + mirrored[:, None]], axis=1
    )
    angle = math.pi * bins / LENGTH
    shift = np.stack([np.cos(angle), np.sin(angle)]).astype(np.float32)
    shift = np.repeat(shift[:, :, None, :], ST, axis=2)
    order = bins.reshape(-1)
    steps = np.outer(order, 2 * np.arange(HALF_LAGS) + 1) % (2 * LENGTH)
    weight = np.where(order == 0, 1.0, 2.0)
    lag_cos = weight[:, None] * np.cos(math.pi * steps / LENGTH)
    lag_cos = lag_cos.reshape(FREQ, 2, 256).transpose(1, 0, 2).astype(ml_dtypes.bfloat16)
    return taper, first, turn, second, shift, lag_cos


def kernel(
    n_sta,
    n_tm,
    x_hbm,
    counts,
    partners,
    tap_hbm,
    first_hbm,
    turn_hbm,
    second_hbm,
    shift_hbm,
    cos_hbm,
    out_ref,
    xv,
    halo,
    tapv,
    firstv,
    turnv,
    secondv,
    shiftv,
    cosv,
    y,
    u,
    vhi,
    vlo,
    white,
    mine,
    got,
    cross0,
    cross12,
    held,
    part0,
    part12,
    recv0,
    recv12,
    load_sem,
    come,
    halo_sem,
    white_send,
    white_recv,
    p0_send,
    p0_recv,
    p12_send,
    p12_recv,
):
    b = lax.axis_index("sta")
    j = lax.axis_index("tm")
    lanes = 2 * HALF_LAGS // n_tm
    group = n_tm // 2

    barrier = pltpu.get_barrier_semaphore()
    neighbours = [(b, lax.rem(j + 1, n_tm)), (b, lax.rem(j + n_tm - 1, n_tm))]
    odd = lax.rem(b, 2)
    ahead = (lax.rem(b + 2, n_sta), j)
    behind = (lax.rem(b + n_sta - 2, n_sta), j)
    sibling = (b + 1 - 2 * odd, j)
    across = (lax.rem(b + n_sta - 3 + 6 * odd, n_sta), j)
    third = (lax.rem(b + n_sta - 3 + 2 * odd, n_sta), j)
    has_ahead, has_behind = b < n_sta - 2, b >= 2
    sends = [has_behind, (odd == 1) | (b >= 4), has_ahead]
    receives = [has_ahead, (odd == 0) | (b < n_sta - 3), has_ahead]
    has_across = ((odd == 1) & (b < n_sta - 3)) | ((odd == 0) & (b >= 4))
    for peer in neighbours + [sibling]:
        pl.semaphore_signal(barrier, inc=1, device_id=peer, device_id_type=MESH)
    for there, peer in ((has_ahead, ahead), (has_behind, behind), (has_across, across)):
        pl.when(there)(
            functools.partial(
                pl.semaphore_signal, barrier, inc=1, device_id=peer, device_id_type=MESH
            )
        )
    arrivals = 3
    for there in (has_ahead, has_behind, has_across):
        arrivals = arrivals + there.astype(jnp.int32)

    for place in range(REACH):

        @pl.when(jnp.logical_not(receives[place]))
        def _():
            for w in range(2):
                for part in range(2):
                    got[w, part, place] = jnp.zeros((2, 128, 128), BF16)

    def pass_on(step):
        for neighbour in neighbours:
            pl.semaphore_signal(
                come.at[step], inc=1, device_id=neighbour, device_id_type=MESH
            )

    loads = []
    for idx, (src, dst) in enumerate(
        [
            (x_hbm, xv),
            (tap_hbm, tapv),
            (first_hbm, firstv),
            (turn_hbm, turnv),
            (second_hbm, secondv),
            (shift_hbm, shiftv),
            (cos_hbm, cosv),
        ]
    ):
        loads.append(pltpu.make_async_copy(src, dst, load_sem.at[idx]))
    for copy in loads[:-1]:
        copy.start()

    loads[0].wait()
    pl.semaphore_wait(barrier, arrivals)
    halo_copies = []
    for part in range(4):
        rows = pl.ds(8 * part, 8)
        copy = pltpu.make_async_remote_copy(
            src_ref=xv.at[rows],
            dst_ref=halo.at[rows],
            send_sem=halo_sem.at[0, part],
            recv_sem=halo_sem.at[1, part],
            device_id=(b, lax.rem(j + n_tm - 1, n_tm)),
            device_id_type=MESH,
        )
        copy.start()
        halo_copies.append(copy)
    pass_on(0)

    station = lax.broadcasted_iota(jnp.int32, (ST, 128), 0)
    live = (station < counts[0]).astype(F32)

    lane = lax.broadcasted_iota(jnp.int32, (ST, 128), 1)
    opposite = jnp.where(lane < 64, (64 - lane) & 63, 191 - lane)

    def by_lane(value, index):
        return jnp.take_along_axis(value, index, axis=1, mode="promise_in_bounds")

    def first_step(frames, begin, end):
        frames = (frames * tapv[begin:end]).reshape((end - begin) * ST, 128)
        at = slice(ST * begin, ST * end)
        high = frames.astype(BF16)
        y[at, 0:128] = high
        y[at, 128:256] = (frames - high.astype(F32)).astype(BF16)
        both = jnp.dot(firstv[0, :, at], y[at, :], preferred_element_type=F32)
        return (
            both[:, 0:128]
            + both[:, 128:256]
            + jnp.dot(firstv[1, :, at], y[at, 0:128], preferred_element_type=F32)
        ).reshape(2 * LIVE_ROWS, ST, 128)

    def total(frames):
        return jnp.sum(jnp.sum(frames, axis=0), axis=1, keepdims=True)

    def turned(row):
        re0, im0 = u[row], u[LIVE_ROWS + row]
        re1, im1 = (u[32], u[LIVE_ROWS + 32]) if row == 0 else (re0, im0)
        c0, s0, c1, s1 = turnv[0, row], turnv[1, row], turnv[2, row], turnv[3, row]
        return (
            re0 * c0 + im0 * s0,
            im0 * c0 - re0 * s0,
            re1 * c1 - im1 * s1,
            -(im1 * c1 + re1 * s1),
        )

    def mirrored_bins(value):
        first = jnp.where(lane == 0, 0.0, by_lane(value[0], opposite))
        return jnp.concatenate([first[None], pltpu.roll(value[1:], 64, 2)])

    def second_step(w, rest=None):
        for i in range(16):
            pair = zip(turned(2 * i), turned(2 * i + 1))
            for block, (upper, lower) in enumerate(pair):
                v = jnp.concatenate([upper, lower], axis=0)
                high = v.astype(BF16)
                vhi[16 * i : 16 * i + 16, 128 * block : 128 * block + 128] = high
                vlo[16 * i : 16 * i + 16, 128 * block : 128 * block + 128] = (
                    v - high.astype(F32)
                ).astype(BF16)
        spec = (
            jnp.dot(vhi[...], secondv[0], preferred_element_type=F32)
            + jnp.dot(vlo[...], secondv[0], preferred_element_type=F32)
            + jnp.dot(vhi[...], secondv[1], preferred_element_type=F32)
        )
        re = spec[:, 0:128].reshape(32, ST, 128)
        im = spec[:, 128:256].reshape(32, ST, 128)
        if rest is not None:
            rest = jnp.where(lane == 0, rest * (LENGTH / 4), 0.0)
            re = jnp.concatenate([(re[0] - 2.0 * rest)[None], (re[1] + rest)[None], re[2:]])
        energy = jnp.sum(re * re + im * im, axis=0)
        energy = (energy + by_lane(energy, 127 - lane)) * (1.0 / BAND)
        scale = live / jnp.sqrt(energy + 1e-06)
        re = (re * scale[None]).reshape(2, 128, 128).astype(BF16)
        im = (im * scale[None]).reshape(2, 128, 128).astype(BF16)
        for part in range(2):
            white[w, part, 0] = re[part]
            white[w, part, 1] = im[part]

    def shifted(w):
        re = white[w, :, 0].astype(F32).reshape(32, ST, 128)
        im = white[w, :, 1].astype(F32).reshape(32, ST, 128)
        left = (re * shiftv[0] + im * shiftv[1], im * shiftv[0] - re * shiftv[1])
        for c in range(2):
            mine[w, c] = left[c]
            mine[w, 2 + c] = mirrored_bins(left[c])

    def start_white(w, part, place, source, to):
        copy = pltpu.make_async_remote_copy(
            src_ref=source,
            dst_ref=got.at[w, part, place],
            send_sem=white_send.at[w, part, place],
            recv_sem=white_recv.at[w, part, place],
            device_id=to,
            device_id_type=MESH,
        )
        pl.when(sends[place])(copy.start)
        return copy

    def send_near(w):
        return [[start_white(w, part, 0, white.at[w, part], behind)] for part in range(2)]

    def send_far(w, copies):
        for part in range(2):
            copies[part].append(start_white(w, part, 1, white.at[w, part], third))

    def hand_on(w, part, copies):
        pl.when(receives[0])(copies[part][0].wait_recv)
        copies[part].append(start_white(w, part, 2, got.at[w, part, 0], sibling))

    def arrive(copies):
        for place in (1, 2):
            pl.when(receives[place])(copies[place].wait_recv)

    for copy in loads[1:-1]:
        copy.wait()
    frames = xv[...]
    u[...] = first_step(frames - (total(frames) * (1.0 / LENGTH))[None], 0, 64)
    second_step(0)
    loads[-1].start()
    sent0 = send_near(0)
    send_far(0, sent0)
    pl.semaphore_wait(come.at[0], 2)
    pass_on(1)
    shifted(0)
    frames = xv[32:64]
    mean = total(frames) * (2.0 / LENGTH)
    u[...] = first_step(frames - mean[None], 0, 32)
    for copy in halo_copies:
        copy.wait()
    inside = (j < n_tm - 1).astype(F32)
    frames = halo[...] * inside - mean[None]
    u[...] += first_step(frames, 32, 64)
    second_step(1, total(frames) * (1.0 / LENGTH))
    sent1 = send_near(1)
    pl.semaphore_wait(come.at[1], 2)
    pass_on(2)
    shifted(1)

    def cross_pair(others, cross, slots, windows, part, i):
        right = others(part, slice(16 * i, 16 * i + 16), windows)
        for half in range(2):
            row = 16 * part + 2 * i + half
            at = slice(128 * (row - 16 * part), 128 * (row - 16 * part) + 128)
            own = slice(8 * half, 8 * half + 8)
            terms = []
            for slot in range(slots):
                terms.append([])
                for pair in right[slot]:
                    values = [value[own] for value in pair]
                    if row == 0:
                        values += [by_lane(value, opposite) for value in values]
                    else:
                        values += [pltpu.roll(value, 64, 1) for value in values]
                    terms[slot].append(values)
            for s in range(0, ST, 2):
                kept = [[], []]
                for t in (s, s + 1):
                    left = [
                        [
                            jnp.broadcast_to(mine[w, c, row, t : t + 1, :], (ST, 128))
                            for c in range(4)
                        ]
                        for w in windows
                    ]
                    for slot in range(slots):
                        re, im = None, None
                        for mine_values, values in zip(left, terms[slot]):
                            a_re, a_im, back_re, back_im = mine_values
                            o_re, o_im, other_re, other_im = values
                            new_re = a_re * o_re + a_im * o_im
                            new_im = back_im * other_re - back_re * other_im
                            re = new_re if re is None else re + new_re
                            im = new_im if im is None else im + new_im
                        kept[0].append(re - im)
                        kept[1].append(re + im)
                for slot in range(slots):
                    for sign in range(2):
                        at_rows = pl.ds((sign * slots + slot) * PAIRS + s * ST, 16)
                        cross[part, at_rows, at] = jnp.concatenate(
                            [kept[sign][slot], kept[sign][slots + slot]], axis=0
                        ).astype(BF16)

    def cross_terms(others, cross, slots, windows, part):
        for i in range(8):
            cross_pair(others, cross, slots, windows, part, i)

    half_bins = FREQ // 2

    def lag_sums(cross, half, part):
        at = slice(half_bins * part, half_bins * part + half_bins)
        return jnp.dot(cross[part], cosv[half, at, :], preferred_element_type=F32)

    def all_sums(cross, half):
        return lag_sums(cross, half, 0) + lag_sums(cross, half, 1)

    def keep_part(sums, half, part):
        rows = sums.shape[0] // 2
        even = (lax.broadcasted_iota(jnp.int32, (rows, 256), 1) & 1) == 0
        minus, plus = sums[:rows], sums[rows:]
        later = jnp.where(even, minus, plus).astype(BF16)
        earlier = jnp.where(even, plus, minus).astype(BF16)
        for e in range(n_tm // 4):
            at = slice(lanes * e, lanes * e + lanes)
            block = half * (n_tm // 4) + e
            part[group + block] = later[:, at]
            part[group - 1 - block] = earlier[:, at]

    def send_part(part, recv, send_sem, recv_sem):
        copies = []
        for d in sorted(range(1, n_tm), key=lambda d: -min(d, n_tm - d)):
            to = lax.rem(j + d, n_tm)
            copy = pltpu.make_async_remote_copy(
                src_ref=part.at[to],
                dst_ref=recv.at[d - 1],
                send_sem=send_sem.at[d - 1],
                recv_sem=recv_sem.at[d - 1],
                device_id=(b, to),
                device_id_type=MESH,
            )
            copy.start()
            copies.append((d, copy))
        return copies

    def own_rows(part, rows, windows):
        return [[[white[w, part, c, rows, :].astype(F32) for c in range(2)] for w in windows]]

    cross_terms(own_rows, cross0, 1, (0, 1), 0)
    send_far(1, sent1)
    hand_on(0, 0, sent0)
    hand_on(0, 1, sent0)
    cross_terms(own_rows, cross0, 1, (0, 1), 1)
    loads[-1].wait()
    pl.semaphore_wait(come.at[2], 2)
    for half in range(2):
        keep_part(all_sums(cross0, half), half, part0)
    terms0 = send_part(part0, recv0, p0_send, p0_recv)

    offsets = (2, 1 + 2 * odd, 3 - 2 * odd)
    takes = [
        [(partners[slot] == b + offset).astype(F32) for offset in offsets]
        for slot in range(1, SLOTS)
    ]

    def chosen(part, rows, windows):
        slots = [[] for _ in takes]
        for w in windows:
            pairs = [[] for _ in takes]
            for c in range(2):
                values = [got[w, part, d, c, rows, :].astype(F32) for d in range(REACH)]
                for pair, take in zip(pairs, takes):
                    pair.append(values[0] * take[0] + values[1] * take[1] + values[2] * take[2])
            for slot, pair in zip(slots, pairs):
                slot.append(pair)
        return slots

    for part in range(2):
        arrive(sent0[part])
        cross_terms(chosen, cross12, SLOTS - 1, (0,), part)
    hand_on(1, 0, sent1)
    hand_on(1, 1, sent1)
    for half in range(2):
        held[half] = all_sums(cross12, half)
    for part in range(2):
        arrive(sent1[part])
        if part == 1:
            for half in range(2):
                held[half] += lag_sums(cross12, half, 0)
        cross_terms(chosen, cross12, SLOTS - 1, (1,), part)
    for half in range(2):
        keep_part(held[half] + lag_sums(cross12, half, 1), half, part12)
    terms12 = send_part(part12, recv12, p12_send, p12_recv)

    at = lax.broadcasted_iota(jnp.int32, (ST, lanes), 1)
    at = jnp.where(j >= group, at, lanes - 1 - at)

    def finish(part, recv, copies):
        series = part[j].astype(F32)
        for d, copy in reversed(copies):
            copy.wait()
            series = series + recv[d - 1].astype(F32)
        blocks = [by_lane(series[r : r + ST], at) for r in range(0, series.shape[0], ST)]
        return jnp.concatenate(blocks, axis=0)

    for copies in sent0 + sent1:
        for place, copy in enumerate(copies):
            pl.when(sends[place])(copy.wait_send)
    own = finish(part0, recv0, terms0)
    pair = lax.broadcasted_iota(jnp.int32, (PAIRS, lanes), 0)
    own = jnp.where((pair >> 3) == (pair & 7), 0.0, own)
    out_ref[0:PAIRS, :] = own
    out_ref[PAIRS : SLOTS * PAIRS, :] = finish(part12, recv12, terms12)


def shards(n_sta, n_tm, traces, station_counts, partners):
    x = traces.reshape(ST, 64, 128).transpose(1, 0, 2)
    consts = [jnp.asarray(table) for table in tables()]
    lanes = 2 * HALF_LAGS // n_tm
    anywhere = pl.BlockSpec(memory_space=pl.ANY)
    scalars = pl.BlockSpec(memory_space=pltpu.SMEM)
    dma = pltpu.SemaphoreType.DMA
    series = pl.pallas_call(
        functools.partial(kernel, n_sta, n_tm),
        out_shape=jax.ShapeDtypeStruct((SLOTS * PAIRS, lanes), F32),
        in_specs=[anywhere, scalars, scalars] + [anywhere] * len(consts),
        out_specs=pl.BlockSpec(memory_space=pltpu.VMEM),
        scratch_shapes=[
            pltpu.VMEM((64, ST, 128), F32),
            pltpu.VMEM((32, ST, 128), F32),
            *[pltpu.VMEM(table.shape, table.dtype) for table in consts],
            pltpu.VMEM((64 * ST, 256), BF16),
            pltpu.VMEM((2 * LIVE_ROWS, ST, 128), F32),
            pltpu.VMEM((256, 512), BF16),
            pltpu.VMEM((256, 512), BF16),
            pltpu.VMEM((2, 2, 2, 128, 128), BF16),
            pltpu.VMEM((2, 4, 32, ST, 128), F32),
            pltpu.VMEM((2, 2, REACH, 2, 128, 128), BF16),
            pltpu.VMEM((2, 2 * PAIRS, FREQ // 2), BF16),
            pltpu.VMEM((2, 4 * PAIRS, FREQ // 2), BF16),
            pltpu.VMEM((2, 4 * PAIRS, 256), F32),
            pltpu.VMEM((n_tm, PAIRS, lanes), BF16),
            pltpu.VMEM((n_tm, 2 * PAIRS, lanes), BF16),
            pltpu.VMEM((n_tm - 1, PAIRS, lanes), BF16),
            pltpu.VMEM((n_tm - 1, 2 * PAIRS, lanes), BF16),
            dma((7,)),
            pltpu.SemaphoreType.REGULAR((n_tm // 2 - 1,)),
            dma((2, 4)),
            dma((2, 2, REACH)),
            dma((2, 2, REACH)),
            dma((n_tm - 1,)),
            dma((n_tm - 1,)),
            dma((n_tm - 1,)),
            dma((n_tm - 1,)),
        ],
        compiler_params=pltpu.CompilerParams(
            collective_id=0, has_side_effects=True, vmem_limit_bytes=VMEM_LIMIT
        ),
    )(x, station_counts, partners.reshape(SLOTS), *consts)
    norm = 1.0 / math.sqrt(2.0 * LENGTH * n_tm)
    return (series * norm).reshape(1, SLOTS, ST, ST, lanes)


def solution(mesh):
    placed = (P("sta", "tm"), P("sta"), P("sta", None))
    return jax.shard_map(
        functools.partial(shards, mesh.shape["sta"], mesh.shape["tm"]),
        mesh=mesh,
        in_specs=placed,
        out_specs=P("sta", None, None, None, "tm"),
        check_vma=False,
    )
```

```python
import functools
import math

import jax
import jax.numpy as jnp
import ml_dtypes
import numpy as np
from jax import lax
from jax.experimental import pallas as pl
from jax.experimental.pallas import tpu as pltpu
from jax.sharding import PartitionSpec as P

MESH = pl.DeviceIdType.MESH
F32 = jnp.float32
BF16 = jnp.bfloat16

ST = 8
FREQ = 4096
LENGTH = 2 * FREQ
BAND = 64
HALF_LAGS = 512
SLOTS = 3
REACH = 3
PAIRS = ST * ST
VMEM_LIMIT = 55100 * 2**10
LIVE_ROWS = 33


def split(table):
    high = table.astype(ml_dtypes.bfloat16)
    low = (table - high.astype(np.float64)).astype(ml_dtypes.bfloat16)
    return np.stack([high, low])


def tables():
    m = np.arange(64)
    q = np.arange(128)
    taper = 0.5 - 0.5 * np.cos(np.arange(LENGTH) * (2.0 * math.pi / LENGTH))
    taper = np.repeat(taper.astype(np.float32).reshape(64, 1, 128), ST, axis=1)
    angle = 2.0 * math.pi * (np.outer(np.arange(LIVE_ROWS), m) % 64) / 64
    first = split(np.kron(np.concatenate([np.cos(angle), -np.sin(angle)]), np.eye(ST)))
    ids = np.arange(32)
    mirrored = np.where(ids == 0, 32, 64 - ids)
    near = 2.0 * math.pi * np.outer(ids, q) / LENGTH
    far = 2.0 * math.pi * np.outer(mirrored, q) / LENGTH
    turn = np.stack([np.cos(near), np.sin(near), np.cos(far), np.sin(far)])
    turn = np.repeat(turn.astype(np.float32)[:, :, None, :], ST, axis=2)
    k = np.arange(BAND)
    angle = 2.0 * math.pi * (np.outer(q, k) % 128) / 128
    cos, sin, none = np.cos(angle), np.sin(angle), np.zeros((128, BAND))
    back_cos, back_sin = cos[:, ::-1], sin[:, ::-1]
    second = np.concatenate(
        [
            np.concatenate([cos, none, -sin, none], axis=1),
            np.concatenate([sin, none, cos, none], axis=1),
            np.concatenate([none, back_cos, none, -back_sin], axis=1),
            np.concatenate([none, back_sin, none, back_cos], axis=1),
        ]
    )
    second = split(second)
    bins = np.concatenate(
        [64 * k[None, :] + ids[:, None], 64 * (63 - k)[None, :] + mirrored[:, None]], axis=1
    )
    angle = math.pi * bins / LENGTH
    shift = np.stack([np.cos(angle), np.sin(angle)]).astype(np.float32)
    shift = np.repeat(shift[:, :, None, :], ST, axis=2)
    order = bins.reshape(-1)
    steps = np.outer(order, 2 * np.arange(HALF_LAGS) + 1) % (2 * LENGTH)
    weight = np.where(order == 0, 1.0, 2.0)
    lag_cos = weight[:, None] * np.cos(math.pi * steps / LENGTH)
    lag_cos = lag_cos.reshape(FREQ, 2, 256).transpose(1, 0, 2).astype(ml_dtypes.bfloat16)
    return taper, first, turn, second, shift, lag_cos


def kernel(
    n_sta,
    n_tm,
    x_hbm,
    counts_hbm,
    partners_hbm,
    tap_hbm,
    first_hbm,
    turn_hbm,
    second_hbm,
    shift_hbm,
    cos_hbm,
    out_ref,
    counts,
    partners,
    xv,
    halo,
    tapv,
    firstv,
    turnv,
    secondv,
    shiftv,
    cosv,
    y,
    u,
    vhi,
    vlo,
    white,
    mine,
    got,
    cross0,
    cross12,
    held,
    part0,
    part12,
    recv0,
    recv12,
    load_sem,
    come,
    halo_sem,
    white_send,
    white_recv,
    p0_send,
    p0_recv,
    p12_send,
    p12_recv,
):
    b = lax.axis_index("sta")
    j = lax.axis_index("tm")
    lanes = 2 * HALF_LAGS // n_tm
    group = n_tm // 2

    barrier = pltpu.get_barrier_semaphore()
    neighbours = [(b, lax.rem(j + 1, n_tm)), (b, lax.rem(j + n_tm - 1, n_tm))]
    odd = lax.rem(b, 2)
    ahead = (lax.rem(b + 2, n_sta), j)
    behind = (lax.rem(b + n_sta - 2, n_sta), j)
    sibling = (b + 1 - 2 * odd, j)
    across = (lax.rem(b + n_sta - 3 + 6 * odd, n_sta), j)
    third = (lax.rem(b + n_sta - 3 + 2 * odd, n_sta), j)
    has_ahead, has_behind = b < n_sta - 2, b >= 2
    sends = [has_behind, (odd == 1) | (b >= 4), has_ahead]
    receives = [has_ahead, (odd == 0) | (b < n_sta - 3), has_ahead]
    has_across = ((odd == 1) & (b < n_sta - 3)) | ((odd == 0) & (b >= 4))
    for peer in neighbours + [sibling]:
        pl.semaphore_signal(barrier, inc=1, device_id=peer, device_id_type=MESH)
    for there, peer in ((has_ahead, ahead), (has_behind, behind), (has_across, across)):
        pl.when(there)(
            functools.partial(
                pl.semaphore_signal, barrier, inc=1, device_id=peer, device_id_type=MESH
            )
        )
    arrivals = 3
    for there in (has_ahead, has_behind, has_across):
        arrivals = arrivals + there.astype(jnp.int32)

    for place in range(REACH):

        @pl.when(jnp.logical_not(receives[place]))
        def _():
            for w in range(2):
                for part in range(2):
                    got[w, part, place] = jnp.zeros((2, 128, 128), BF16)

    def pass_on(step):
        for neighbour in neighbours:
            pl.semaphore_signal(
                come.at[step], inc=1, device_id=neighbour, device_id_type=MESH
            )

    loads = []
    for idx, (src, dst) in enumerate(
        [
            (x_hbm, xv),
            (counts_hbm, counts),
            (partners_hbm, partners),
            (tap_hbm, tapv),
            (first_hbm, firstv),
            (turn_hbm, turnv),
            (second_hbm, secondv),
            (shift_hbm, shiftv),
            (cos_hbm, cosv),
        ]
    ):
        loads.append(pltpu.make_async_copy(src, dst, load_sem.at[idx]))
    for copy in loads[:-1]:
        copy.start()

    loads[0].wait()
    pl.semaphore_wait(barrier, arrivals)
    halo_copies = []
    for part in range(4):
        rows = pl.ds(8 * part, 8)
        copy = pltpu.make_async_remote_copy(
            src_ref=xv.at[rows],
            dst_ref=halo.at[rows],
            send_sem=halo_sem.at[0, part],
            recv_sem=halo_sem.at[1, part],
            device_id=(b, lax.rem(j + n_tm - 1, n_tm)),
            device_id_type=MESH,
        )
        copy.start()
        halo_copies.append(copy)
    pass_on(0)

    loads[1].wait()
    loads[2].wait()
    station = lax.broadcasted_iota(jnp.int32, (ST, 128), 0)
    live = (station < counts[0]).astype(F32)

    lane = lax.broadcasted_iota(jnp.int32, (ST, 128), 1)
    opposite = jnp.where(lane < 64, (64 - lane) & 63, 191 - lane)

    def by_lane(value, index):
        return jnp.take_along_axis(value, index, axis=1, mode="promise_in_bounds")

    def first_step(frames, begin, end):
        frames = (frames * tapv[begin:end]).reshape((end - begin) * ST, 128)
        at = slice(ST * begin, ST * end)
        high = frames.astype(BF16)
        y[at, 0:128] = high
        y[at, 128:256] = (frames - high.astype(F32)).astype(BF16)
        both = jnp.dot(firstv[0, :, at], y[at, :], preferred_element_type=F32)
        return (
            both[:, 0:128]
            + both[:, 128:256]
            + jnp.dot(firstv[1, :, at], y[at, 0:128], preferred_element_type=F32)
        ).reshape(2 * LIVE_ROWS, ST, 128)

    def total(frames):
        return jnp.sum(jnp.sum(frames, axis=0), axis=1, keepdims=True)

    def turned(row):
        re0, im0 = u[row], u[LIVE_ROWS + row]
        re1, im1 = (u[32], u[LIVE_ROWS + 32]) if row == 0 else (re0, im0)
        c0, s0, c1, s1 = turnv[0, row], turnv[1, row], turnv[2, row], turnv[3, row]
        return (
            re0 * c0 + im0 * s0,
            im0 * c0 - re0 * s0,
            re1 * c1 - im1 * s1,
            -(im1 * c1 + re1 * s1),
        )

    def mirrored_bins(value):
        first = jnp.where(lane == 0, 0.0, by_lane(value[0], opposite))
        return jnp.concatenate([first[None], pltpu.roll(value[1:], 64, 2)])

    def second_step(w, rest=None):
        for i in range(16):
            pair = zip(turned(2 * i), turned(2 * i + 1))
            for block, (upper, lower) in enumerate(pair):
                v = jnp.concatenate([upper, lower], axis=0)
                high = v.astype(BF16)
                vhi[16 * i : 16 * i + 16, 128 * block : 128 * block + 128] = high
                vlo[16 * i : 16 * i + 16, 128 * block : 128 * block + 128] = (
                    v - high.astype(F32)
                ).astype(BF16)
        spec = (
            jnp.dot(vhi[...], secondv[0], preferred_element_type=F32)
            + jnp.dot(vlo[...], secondv[0], preferred_element_type=F32)
            + jnp.dot(vhi[...], secondv[1], preferred_element_type=F32)
        )
        re = spec[:, 0:128].reshape(32, ST, 128)
        im = spec[:, 128:256].reshape(32, ST, 128)
        if rest is not None:
            rest = jnp.where(lane == 0, rest * (LENGTH / 4), 0.0)
            re = jnp.concatenate([(re[0] - 2.0 * rest)[None], (re[1] + rest)[None], re[2:]])
        energy = jnp.sum(re * re + im * im, axis=0)
        energy = (energy + by_lane(energy, 127 - lane)) * (1.0 / BAND)
        scale = live / jnp.sqrt(energy + 1e-06)
        re = (re * scale[None]).reshape(2, 128, 128).astype(BF16)
        im = (im * scale[None]).reshape(2, 128, 128).astype(BF16)
        for part in range(2):
            white[w, part, 0] = re[part]
            white[w, part, 1] = im[part]

    def shifted(w):
        re = white[w, :, 0].astype(F32).reshape(32, ST, 128)
        im = white[w, :, 1].astype(F32).reshape(32, ST, 128)
        left = (re * shiftv[0] + im * shiftv[1], im * shiftv[0] - re * shiftv[1])
        for c in range(2):
            mine[w, c] = left[c]
            mine[w, 2 + c] = mirrored_bins(left[c])

    def start_white(w, part, place, source, to):
        copy = pltpu.make_async_remote_copy(
            src_ref=source,
            dst_ref=got.at[w, part, place],
            send_sem=white_send.at[w, part, place],
            recv_sem=white_recv.at[w, part, place],
            device_id=to,
            device_id_type=MESH,
        )
        pl.when(sends[place])(copy.start)
        return copy

    def send_near(w):
        return [[start_white(w, part, 0, white.at[w, part], behind)] for part in range(2)]

    def send_far(w, copies):
        for part in range(2):
            copies[part].append(start_white(w, part, 1, white.at[w, part], third))

    def hand_on(w, part, copies):
        pl.when(receives[0])(copies[part][0].wait_recv)
        copies[part].append(start_white(w, part, 2, got.at[w, part, 0], sibling))

    def arrive(copies):
        for place in (1, 2):
            pl.when(receives[place])(copies[place].wait_recv)

    for copy in loads[3:-1]:
        copy.wait()
    frames = xv[...]
    u[...] = first_step(frames - (total(frames) * (1.0 / LENGTH))[None], 0, 64)
    second_step(0)
    loads[-1].start()
    sent0 = send_near(0)
    send_far(0, sent0)
    pl.semaphore_wait(come.at[0], 2)
    pass_on(1)
    shifted(0)
    frames = xv[32:64]
    mean = total(frames) * (2.0 / LENGTH)
    u[...] = first_step(frames - mean[None], 0, 32)
    for copy in halo_copies:
        copy.wait()
    inside = (j < n_tm - 1).astype(F32)
    frames = halo[...] * inside - mean[None]
    u[...] += first_step(frames, 32, 64)
    second_step(1, total(frames) * (1.0 / LENGTH))
    sent1 = send_near(1)
    pl.semaphore_wait(come.at[1], 2)
    pass_on(2)
    shifted(1)

    def cross_pair(others, cross, slots, windows, part, i):
        right = others(part, slice(16 * i, 16 * i + 16), windows)
        for half in range(2):
            row = 16 * part + 2 * i + half
            at = slice(128 * (row - 16 * part), 128 * (row - 16 * part) + 128)
            own = slice(8 * half, 8 * half + 8)
            terms = []
            for slot in range(slots):
                terms.append([])
                for pair in right[slot]:
                    values = [value[own] for value in pair]
                    if row == 0:
                        values += [by_lane(value, opposite) for value in values]
                    else:
                        values += [pltpu.roll(value, 64, 1) for value in values]
                    terms[slot].append(values)
            for s in range(0, ST, 2):
                kept = [[], []]
                for t in (s, s + 1):
                    left = [
                        [
                            jnp.broadcast_to(mine[w, c, row, t : t + 1, :], (ST, 128))
                            for c in range(4)
                        ]
                        for w in windows
                    ]
                    for slot in range(slots):
                        re, im = None, None
                        for mine_values, values in zip(left, terms[slot]):
                            a_re, a_im, back_re, back_im = mine_values
                            o_re, o_im, other_re, other_im = values
                            new_re = a_re * o_re + a_im * o_im
                            new_im = back_im * other_re - back_re * other_im
                            re = new_re if re is None else re + new_re
                            im = new_im if im is None else im + new_im
                        kept[0].append(re - im)
                        kept[1].append(re + im)
                for slot in range(slots):
                    for sign in range(2):
                        at_rows = pl.ds((sign * slots + slot) * PAIRS + s * ST, 16)
                        cross[part, at_rows, at] = jnp.concatenate(
                            [kept[sign][slot], kept[sign][slots + slot]], axis=0
                        ).astype(BF16)

    def cross_terms(others, cross, slots, windows, part):
        for i in range(8):
            cross_pair(others, cross, slots, windows, part, i)

    half_bins = FREQ // 2

    def lag_sums(cross, half, part):
        at = slice(half_bins * part, half_bins * part + half_bins)
        return jnp.dot(cross[part], cosv[half, at, :], preferred_element_type=F32)

    def all_sums(cross, half):
        return lag_sums(cross, half, 0) + lag_sums(cross, half, 1)

    def keep_part(sums, half, part):
        rows = sums.shape[0] // 2
        even = (lax.broadcasted_iota(jnp.int32, (rows, 256), 1) & 1) == 0
        minus, plus = sums[:rows], sums[rows:]
        later = jnp.where(even, minus, plus).astype(BF16)
        earlier = jnp.where(even, plus, minus).astype(BF16)
        for e in range(n_tm // 4):
            at = slice(lanes * e, lanes * e + lanes)
            block = half * (n_tm // 4) + e
            part[group + block] = later[:, at]
            part[group - 1 - block] = earlier[:, at]

    def send_part(part, recv, send_sem, recv_sem):
        copies = []
        for d in sorted(range(1, n_tm), key=lambda d: -min(d, n_tm - d)):
            to = lax.rem(j + d, n_tm)
            copy = pltpu.make_async_remote_copy(
                src_ref=part.at[to],
                dst_ref=recv.at[d - 1],
                send_sem=send_sem.at[d - 1],
                recv_sem=recv_sem.at[d - 1],
                device_id=(b, to),
                device_id_type=MESH,
            )
            copy.start()
            copies.append((d, copy))
        return copies

    def own_rows(part, rows, windows):
        return [[[white[w, part, c, rows, :].astype(F32) for c in range(2)] for w in windows]]

    cross_terms(own_rows, cross0, 1, (0, 1), 0)
    send_far(1, sent1)
    hand_on(0, 0, sent0)
    hand_on(0, 1, sent0)
    cross_terms(own_rows, cross0, 1, (0, 1), 1)
    loads[-1].wait()
    pl.semaphore_wait(come.at[2], 2)
    for half in range(2):
        keep_part(all_sums(cross0, half), half, part0)
    terms0 = send_part(part0, recv0, p0_send, p0_recv)

    offsets = (2, 1 + 2 * odd, 3 - 2 * odd)
    takes = [
        [(partners[slot] == b + offset).astype(F32) for offset in offsets]
        for slot in range(1, SLOTS)
    ]

    def chosen(part, rows, windows):
        slots = [[] for _ in takes]
        for w in windows:
            pairs = [[] for _ in takes]
            for c in range(2):
                values = [got[w, part, d, c, rows, :].astype(F32) for d in range(REACH)]
                for pair, take in zip(pairs, takes):
                    pair.append(values[0] * take[0] + values[1] * take[1] + values[2] * take[2])
            for slot, pair in zip(slots, pairs):
                slot.append(pair)
        return slots

    for part in range(2):
        arrive(sent0[part])
        cross_terms(chosen, cross12, SLOTS - 1, (0,), part)
    hand_on(1, 0, sent1)
    hand_on(1, 1, sent1)
    for half in range(2):
        held[half] = all_sums(cross12, half)
    for part in range(2):
        arrive(sent1[part])
        if part == 1:
            for half in range(2):
                held[half] += lag_sums(cross12, half, 0)
        cross_terms(chosen, cross12, SLOTS - 1, (1,), part)
    for half in range(2):
        keep_part(held[half] + lag_sums(cross12, half, 1), half, part12)
    terms12 = send_part(part12, recv12, p12_send, p12_recv)

    at = lax.broadcasted_iota(jnp.int32, (ST, lanes), 1)
    at = jnp.where(j >= group, at, lanes - 1 - at)

    def finish(part, recv, copies):
        series = part[j].astype(F32)
        for d, copy in reversed(copies):
            copy.wait()
            series = series + recv[d - 1].astype(F32)
        blocks = [by_lane(series[r : r + ST], at) for r in range(0, series.shape[0], ST)]
        return jnp.concatenate(blocks, axis=0)

    for copies in sent0 + sent1:
        for place, copy in enumerate(copies):
            pl.when(sends[place])(copy.wait_send)
    own = finish(part0, recv0, terms0)
    pair = lax.broadcasted_iota(jnp.int32, (PAIRS, lanes), 0)
    own = jnp.where((pair >> 3) == (pair & 7), 0.0, own)
    out_ref[0:PAIRS, :] = own
    out_ref[PAIRS : SLOTS * PAIRS, :] = finish(part12, recv12, terms12)


def shards(n_sta, n_tm, traces, station_counts, partners):
    x = traces.reshape(ST, 64, 128).transpose(1, 0, 2)
    consts = [jnp.asarray(table) for table in tables()]
    lanes = 2 * HALF_LAGS // n_tm
    anywhere = pl.BlockSpec(memory_space=pl.ANY)
    dma = pltpu.SemaphoreType.DMA
    series = pl.pallas_call(
        functools.partial(kernel, n_sta, n_tm),
        out_shape=jax.ShapeDtypeStruct((SLOTS * PAIRS, lanes), F32),
        in_specs=[anywhere] * (3 + len(consts)),
        out_specs=pl.BlockSpec(memory_space=pltpu.VMEM),
        scratch_shapes=[
            pltpu.SMEM((1,), jnp.int32),
            pltpu.SMEM((SLOTS,), jnp.int32),
            pltpu.VMEM((64, ST, 128), F32),
            pltpu.VMEM((32, ST, 128), F32),
            *[pltpu.VMEM(table.shape, table.dtype) for table in consts],
            pltpu.VMEM((64 * ST, 256), BF16),
            pltpu.VMEM((2 * LIVE_ROWS, ST, 128), F32),
            pltpu.VMEM((256, 512), BF16),
            pltpu.VMEM((256, 512), BF16),
            pltpu.VMEM((2, 2, 2, 128, 128), BF16),
            pltpu.VMEM((2, 4, 32, ST, 128), F32),
            pltpu.VMEM((2, 2, REACH, 2, 128, 128), BF16),
            pltpu.VMEM((2, 2 * PAIRS, FREQ // 2), BF16),
            pltpu.VMEM((2, 4 * PAIRS, FREQ // 2), BF16),
            pltpu.VMEM((2, 4 * PAIRS, 256), F32),
            pltpu.VMEM((n_tm, PAIRS, lanes), BF16),
            pltpu.VMEM((n_tm, 2 * PAIRS, lanes), BF16),
            pltpu.VMEM((n_tm - 1, PAIRS, lanes), BF16),
            pltpu.VMEM((n_tm - 1, 2 * PAIRS, lanes), BF16),
            dma((9,)),
            pltpu.SemaphoreType.REGULAR((n_tm // 2 - 1,)),
            dma((2, 4)),
            dma((2, 2, REACH)),
            dma((2, 2, REACH)),
            dma((n_tm - 1,)),
            dma((n_tm - 1,)),
            dma((n_tm - 1,)),
            dma((n_tm - 1,)),
        ],
        compiler_params=pltpu.CompilerParams(
            collective_id=0, has_side_effects=True, vmem_limit_bytes=VMEM_LIMIT
        ),
    )(x, station_counts, partners.reshape(SLOTS), *consts)
    norm = 1.0 / math.sqrt(2.0 * LENGTH * n_tm)
    return (series * norm).reshape(1, SLOTS, ST, ST, lanes)


def solution(mesh):
    placed = (P("sta", "tm"), P("sta"), P("sta", None))
    return jax.shard_map(
        functools.partial(shards, mesh.shape["sta"], mesh.shape["tm"]),
        mesh=mesh,
        in_specs=placed,
        out_specs=P("sta", None, None, None, "tm"),
        check_vma=False,
    )
```

```python
import functools
import math

import jax
import jax.numpy as jnp
import ml_dtypes
import numpy as np
from jax import lax
from jax.experimental import pallas as pl
from jax.experimental.pallas import tpu as pltpu
from jax.sharding import PartitionSpec as P

MESH = pl.DeviceIdType.MESH
F32 = jnp.float32
BF16 = jnp.bfloat16

ST = 8
FREQ = 4096
LENGTH = 2 * FREQ
BAND = 64
HALF_LAGS = 512
SLOTS = 3
REACH = 3
PAIRS = ST * ST
VMEM_LIMIT = 55100 * 2**10
LIVE_ROWS = 33


def split(table):
    high = table.astype(ml_dtypes.bfloat16)
    low = (table - high.astype(np.float64)).astype(ml_dtypes.bfloat16)
    return np.stack([high, low])


def tables():
    m = np.arange(64)
    q = np.arange(128)
    taper = 0.5 - 0.5 * np.cos(np.arange(LENGTH) * (2.0 * math.pi / LENGTH))
    taper = np.repeat(taper.astype(np.float32).reshape(64, 1, 128), ST, axis=1)
    angle = 2.0 * math.pi * (np.outer(np.arange(LIVE_ROWS), m) % 64) / 64
    first = split(np.kron(np.concatenate([np.cos(angle), -np.sin(angle)]), np.eye(ST)))
    ids = np.arange(32)
    mirrored = np.where(ids == 0, 32, 64 - ids)
    near = 2.0 * math.pi * np.outer(ids, q) / LENGTH
    far = 2.0 * math.pi * np.outer(mirrored, q) / LENGTH
    turn = np.stack([np.cos(near), np.sin(near), np.cos(far), np.sin(far)])
    turn = np.repeat(turn.astype(np.float32)[:, :, None, :], ST, axis=2)
    k = np.arange(BAND)
    angle = 2.0 * math.pi * (np.outer(q, k) % 128) / 128
    cos, sin, none = np.cos(angle), np.sin(angle), np.zeros((128, BAND))
    back_cos, back_sin = cos[:, ::-1], sin[:, ::-1]
    second = np.concatenate(
        [
            np.concatenate([cos, none, -sin, none], axis=1),
            np.concatenate([sin, none, cos, none], axis=1),
            np.concatenate([none, back_cos, none, -back_sin], axis=1),
            np.concatenate([none, back_sin, none, back_cos], axis=1),
        ]
    )
    second = split(second)
    bins = np.concatenate(
        [64 * k[None, :] + ids[:, None], 64 * (63 - k)[None, :] + mirrored[:, None]], axis=1
    )
    angle = math.pi * bins / LENGTH
    shift = np.stack([np.cos(angle), np.sin(angle)]).astype(np.float32)
    shift = np.repeat(shift[:, :, None, :], ST, axis=2)
    order = bins.reshape(-1)
    steps = np.outer(order, 2 * np.arange(HALF_LAGS) + 1) % (2 * LENGTH)
    weight = np.where(order == 0, 1.0, 2.0)
    lag_cos = weight[:, None] * np.cos(math.pi * steps / LENGTH)
    lag_cos = lag_cos.reshape(FREQ, 2, 256).transpose(1, 0, 2).astype(ml_dtypes.bfloat16)
    return taper, first, turn, second, shift, lag_cos


def kernel(
    n_sta,
    n_tm,
    x_hbm,
    counts_hbm,
    partners_hbm,
    tap_hbm,
    first_hbm,
    turn_hbm,
    second_hbm,
    shift_hbm,
    cos_hbm,
    out_ref,
    counts,
    partners,
    xv,
    halo,
    tapv,
    firstv,
    turnv,
    secondv,
    shiftv,
    cosv,
    y,
    u,
    vhi,
    vlo,
    white,
    mine,
    got,
    cross0,
    cross12,
    held,
    part0,
    part12,
    recv0,
    recv12,
    load_sem,
    come,
    halo_sem,
    white_send,
    white_recv,
    p0_send,
    p0_recv,
    p12_send,
    p12_recv,
):
    b = lax.axis_index("sta")
    j = lax.axis_index("tm")
    lanes = 2 * HALF_LAGS // n_tm
    group = n_tm // 2

    barrier = pltpu.get_barrier_semaphore()
    neighbours = [(b, lax.rem(j + 1, n_tm)), (b, lax.rem(j + n_tm - 1, n_tm))]
    odd = lax.rem(b, 2)
    ahead = (lax.rem(b + 2, n_sta), j)
    behind = (lax.rem(b + n_sta - 2, n_sta), j)
    sibling = (b + 1 - 2 * odd, j)
    across = (lax.rem(b + n_sta - 3 + 6 * odd, n_sta), j)
    third = (lax.rem(b + n_sta - 3 + 2 * odd, n_sta), j)
    has_ahead, has_behind = b < n_sta - 2, b >= 2
    sends = [has_behind, (odd == 1) | (b >= 4), has_ahead]
    receives = [has_ahead, (odd == 0) | (b < n_sta - 3), has_ahead]
    has_across = ((odd == 1) & (b < n_sta - 3)) | ((odd == 0) & (b >= 4))
    for peer in neighbours + [sibling]:
        pl.semaphore_signal(barrier, inc=1, device_id=peer, device_id_type=MESH)
    for there, peer in ((has_ahead, ahead), (has_behind, behind), (has_across, across)):
        pl.when(there)(
            functools.partial(
                pl.semaphore_signal, barrier, inc=1, device_id=peer, device_id_type=MESH
            )
        )
    arrivals = 3
    for there in (has_ahead, has_behind, has_across):
        arrivals = arrivals + there.astype(jnp.int32)

    for place in range(REACH):

        @pl.when(jnp.logical_not(receives[place]))
        def _():
            for w in range(2):
                for part in range(2):
                    got[w, part, place] = jnp.zeros((2, 128, 128), BF16)

    def pass_on(step):
        for neighbour in neighbours:
            pl.semaphore_signal(
                come.at[step], inc=1, device_id=neighbour, device_id_type=MESH
            )

    loads = []
    for idx, (src, dst) in enumerate(
        [
            (x_hbm, xv),
            (counts_hbm, counts),
            (partners_hbm, partners),
            (tap_hbm, tapv),
            (first_hbm, firstv),
            (turn_hbm, turnv),
            (second_hbm, secondv),
            (shift_hbm, shiftv),
            (cos_hbm, cosv),
        ]
    ):
        loads.append(pltpu.make_async_copy(src, dst, load_sem.at[idx]))
    for copy in loads[:-1]:
        copy.start()

    def tapered(frames, begin, end):
        frames = (frames * tapv[begin:end]).reshape((end - begin) * ST, 128)
        at = slice(ST * begin, ST * end)
        high = frames.astype(BF16)
        y[at, 0:128] = high
        y[at, 128:256] = (frames - high.astype(F32)).astype(BF16)

    def first_step(begin, end):
        at = slice(ST * begin, ST * end)
        both = jnp.dot(firstv[0, :, at], y[at, :], preferred_element_type=F32)
        return (
            both[:, 0:128]
            + both[:, 128:256]
            + jnp.dot(firstv[1, :, at], y[at, 0:128], preferred_element_type=F32)
        ).reshape(2 * LIVE_ROWS, ST, 128)

    def total(frames):
        return jnp.sum(jnp.sum(frames, axis=0), axis=1, keepdims=True)

    loads[0].wait()
    loads[3].wait()
    frames = xv[...]
    tapered(frames - (total(frames) * (1.0 / LENGTH))[None], 0, 64)
    pl.semaphore_wait(barrier, arrivals)
    halo_copies = []
    for part in range(4):
        rows = pl.ds(8 * part, 8)
        copy = pltpu.make_async_remote_copy(
            src_ref=xv.at[rows],
            dst_ref=halo.at[rows],
            send_sem=halo_sem.at[0, part],
            recv_sem=halo_sem.at[1, part],
            device_id=(b, lax.rem(j + n_tm - 1, n_tm)),
            device_id_type=MESH,
        )
        copy.start()
        halo_copies.append(copy)
    pass_on(0)

    loads[1].wait()
    loads[2].wait()
    station = lax.broadcasted_iota(jnp.int32, (ST, 128), 0)
    live = (station < counts[0]).astype(F32)

    lane = lax.broadcasted_iota(jnp.int32, (ST, 128), 1)
    opposite = jnp.where(lane < 64, (64 - lane) & 63, 191 - lane)

    def by_lane(value, index):
        return jnp.take_along_axis(value, index, axis=1, mode="promise_in_bounds")

    def turned(row):
        re0, im0 = u[row], u[LIVE_ROWS + row]
        re1, im1 = (u[32], u[LIVE_ROWS + 32]) if row == 0 else (re0, im0)
        c0, s0, c1, s1 = turnv[0, row], turnv[1, row], turnv[2, row], turnv[3, row]
        return (
            re0 * c0 + im0 * s0,
            im0 * c0 - re0 * s0,
            re1 * c1 - im1 * s1,
            -(im1 * c1 + re1 * s1),
        )

    def mirrored_bins(value):
        first = jnp.where(lane == 0, 0.0, by_lane(value[0], opposite))
        return jnp.concatenate([first[None], pltpu.roll(value[1:], 64, 2)])

    def second_step(w, rest=None):
        for i in range(16):
            pair = zip(turned(2 * i), turned(2 * i + 1))
            for block, (upper, lower) in enumerate(pair):
                v = jnp.concatenate([upper, lower], axis=0)
                high = v.astype(BF16)
                vhi[16 * i : 16 * i + 16, 128 * block : 128 * block + 128] = high
                vlo[16 * i : 16 * i + 16, 128 * block : 128 * block + 128] = (
                    v - high.astype(F32)
                ).astype(BF16)
        spec = (
            jnp.dot(vhi[...], secondv[0], preferred_element_type=F32)
            + jnp.dot(vlo[...], secondv[0], preferred_element_type=F32)
            + jnp.dot(vhi[...], secondv[1], preferred_element_type=F32)
        )
        re = spec[:, 0:128].reshape(32, ST, 128)
        im = spec[:, 128:256].reshape(32, ST, 128)
        if rest is not None:
            rest = jnp.where(lane == 0, rest * (LENGTH / 4), 0.0)
            re = jnp.concatenate([(re[0] - 2.0 * rest)[None], (re[1] + rest)[None], re[2:]])
        energy = jnp.sum(re * re + im * im, axis=0)
        energy = (energy + by_lane(energy, 127 - lane)) * (1.0 / BAND)
        scale = live / jnp.sqrt(energy + 1e-06)
        re = (re * scale[None]).reshape(2, 128, 128).astype(BF16)
        im = (im * scale[None]).reshape(2, 128, 128).astype(BF16)
        for part in range(2):
            white[w, part, 0] = re[part]
            white[w, part, 1] = im[part]

    def shifted(w):
        re = white[w, :, 0].astype(F32).reshape(32, ST, 128)
        im = white[w, :, 1].astype(F32).reshape(32, ST, 128)
        left = (re * shiftv[0] + im * shiftv[1], im * shiftv[0] - re * shiftv[1])
        for c in range(2):
            mine[w, c] = left[c]
            mine[w, 2 + c] = mirrored_bins(left[c])

    def start_white(w, part, place, source, to):
        copy = pltpu.make_async_remote_copy(
            src_ref=source,
            dst_ref=got.at[w, part, place],
            send_sem=white_send.at[w, part, place],
            recv_sem=white_recv.at[w, part, place],
            device_id=to,
            device_id_type=MESH,
        )
        pl.when(sends[place])(copy.start)
        return copy

    def send_near(w):
        return [[start_white(w, part, 0, white.at[w, part], behind)] for part in range(2)]

    def send_far(w, copies):
        for part in range(2):
            copies[part].append(start_white(w, part, 1, white.at[w, part], third))

    def hand_on(w, part, copies):
        pl.when(receives[0])(copies[part][0].wait_recv)
        copies[part].append(start_white(w, part, 2, got.at[w, part, 0], sibling))

    def arrive(copies):
        for place in (1, 2):
            pl.when(receives[place])(copies[place].wait_recv)

    loads[4].wait()
    u[...] = first_step(0, 64)
    loads[5].wait()
    loads[6].wait()
    second_step(0)
    loads[-1].start()
    sent0 = send_near(0)
    send_far(0, sent0)
    pl.semaphore_wait(come.at[0], 2)
    pass_on(1)
    loads[7].wait()
    shifted(0)
    frames = xv[32:64]
    mean = total(frames) * (2.0 / LENGTH)
    tapered(frames - mean[None], 0, 32)
    u[...] = first_step(0, 32)
    for copy in halo_copies:
        copy.wait()
    inside = (j < n_tm - 1).astype(F32)
    frames = halo[...] * inside - mean[None]
    tapered(frames, 32, 64)
    u[...] += first_step(32, 64)
    second_step(1, total(frames) * (1.0 / LENGTH))
    sent1 = send_near(1)
    pl.semaphore_wait(come.at[1], 2)
    pass_on(2)
    shifted(1)

    def cross_pair(others, cross, slots, windows, part, i):
        right = others(part, slice(16 * i, 16 * i + 16), windows)
        for half in range(2):
            row = 16 * part + 2 * i + half
            at = slice(128 * (row - 16 * part), 128 * (row - 16 * part) + 128)
            own = slice(8 * half, 8 * half + 8)
            terms = []
            for slot in range(slots):
                terms.append([])
                for pair in right[slot]:
                    values = [value[own] for value in pair]
                    if row == 0:
                        values += [by_lane(value, opposite) for value in values]
                    else:
                        values += [pltpu.roll(value, 64, 1) for value in values]
                    terms[slot].append(values)
            for s in range(0, ST, 2):
                kept = [[], []]
                for t in (s, s + 1):
                    left = [
                        [
                            jnp.broadcast_to(mine[w, c, row, t : t + 1, :], (ST, 128))
                            for c in range(4)
                        ]
                        for w in windows
                    ]
                    for slot in range(slots):
                        re, im = None, None
                        for mine_values, values in zip(left, terms[slot]):
                            a_re, a_im, back_re, back_im = mine_values
                            o_re, o_im, other_re, other_im = values
                            new_re = a_re * o_re + a_im * o_im
                            new_im = back_im * other_re - back_re * other_im
                            re = new_re if re is None else re + new_re
                            im = new_im if im is None else im + new_im
                        kept[0].append(re - im)
                        kept[1].append(re + im)
                for slot in range(slots):
                    for sign in range(2):
                        at_rows = pl.ds((sign * slots + slot) * PAIRS + s * ST, 16)
                        cross[part, at_rows, at] = jnp.concatenate(
                            [kept[sign][slot], kept[sign][slots + slot]], axis=0
                        ).astype(BF16)

    def cross_terms(others, cross, slots, windows, part):
        for i in range(8):
            cross_pair(others, cross, slots, windows, part, i)

    half_bins = FREQ // 2

    def lag_sums(cross, half, part):
        at = slice(half_bins * part, half_bins * part + half_bins)
        return jnp.dot(cross[part], cosv[half, at, :], preferred_element_type=F32)

    def all_sums(cross, half):
        return lag_sums(cross, half, 0) + lag_sums(cross, half, 1)

    def keep_part(sums, half, part):
        rows = sums.shape[0] // 2
        even = (lax.broadcasted_iota(jnp.int32, (rows, 256), 1) & 1) == 0
        minus, plus = sums[:rows], sums[rows:]
        later = jnp.where(even, minus, plus).astype(BF16)
        earlier = jnp.where(even, plus, minus).astype(BF16)
        for e in range(n_tm // 4):
            at = slice(lanes * e, lanes * e + lanes)
            block = half * (n_tm // 4) + e
            part[group + block] = later[:, at]
            part[group - 1 - block] = earlier[:, at]

    def send_part(part, recv, send_sem, recv_sem):
        copies = []
        for d in sorted(range(1, n_tm), key=lambda d: -min(d, n_tm - d)):
            to = lax.rem(j + d, n_tm)
            copy = pltpu.make_async_remote_copy(
                src_ref=part.at[to],
                dst_ref=recv.at[d - 1],
                send_sem=send_sem.at[d - 1],
                recv_sem=recv_sem.at[d - 1],
                device_id=(b, to),
                device_id_type=MESH,
            )
            copy.start()
            copies.append((d, copy))
        return copies

    def own_rows(part, rows, windows):
        return [[[white[w, part, c, rows, :].astype(F32) for c in range(2)] for w in windows]]

    cross_terms(own_rows, cross0, 1, (0, 1), 0)
    send_far(1, sent1)
    hand_on(0, 0, sent0)
    hand_on(0, 1, sent0)
    cross_terms(own_rows, cross0, 1, (0, 1), 1)
    loads[-1].wait()
    pl.semaphore_wait(come.at[2], 2)
    for half in range(2):
        keep_part(all_sums(cross0, half), half, part0)
    terms0 = send_part(part0, recv0, p0_send, p0_recv)

    offsets = (2, 1 + 2 * odd, 3 - 2 * odd)
    takes = [
        [(partners[slot] == b + offset).astype(F32) for offset in offsets]
        for slot in range(1, SLOTS)
    ]

    def chosen(part, rows, windows):
        slots = [[] for _ in takes]
        for w in windows:
            pairs = [[] for _ in takes]
            for c in range(2):
                values = [got[w, part, d, c, rows, :].astype(F32) for d in range(REACH)]
                for pair, take in zip(pairs, takes):
                    pair.append(values[0] * take[0] + values[1] * take[1] + values[2] * take[2])
            for slot, pair in zip(slots, pairs):
                slot.append(pair)
        return slots

    for part in range(2):
        arrive(sent0[part])
        cross_terms(chosen, cross12, SLOTS - 1, (0,), part)
    hand_on(1, 0, sent1)
    hand_on(1, 1, sent1)
    for half in range(2):
        held[half] = all_sums(cross12, half)
    for part in range(2):
        arrive(sent1[part])
        if part == 1:
            for half in range(2):
                held[half] += lag_sums(cross12, half, 0)
        cross_terms(chosen, cross12, SLOTS - 1, (1,), part)
    for half in range(2):
        keep_part(held[half] + lag_sums(cross12, half, 1), half, part12)
    terms12 = send_part(part12, recv12, p12_send, p12_recv)

    at = lax.broadcasted_iota(jnp.int32, (ST, lanes), 1)
    at = jnp.where(j >= group, at, lanes - 1 - at)

    def finish(part, recv, copies):
        series = part[j].astype(F32)
        for d, copy in reversed(copies):
            copy.wait()
            series = series + recv[d - 1].astype(F32)
        blocks = [by_lane(series[r : r + ST], at) for r in range(0, series.shape[0], ST)]
        return jnp.concatenate(blocks, axis=0)

    for copies in sent0 + sent1:
        for place, copy in enumerate(copies):
            pl.when(sends[place])(copy.wait_send)
    own = finish(part0, recv0, terms0)
    pair = lax.broadcasted_iota(jnp.int32, (PAIRS, lanes), 0)
    own = jnp.where((pair >> 3) == (pair & 7), 0.0, own)
    out_ref[0:PAIRS, :] = own
    out_ref[PAIRS : SLOTS * PAIRS, :] = finish(part12, recv12, terms12)


def shards(n_sta, n_tm, traces, station_counts, partners):
    x = traces.reshape(ST, 64, 128).transpose(1, 0, 2)
    consts = [jnp.asarray(table) for table in tables()]
    lanes = 2 * HALF_LAGS // n_tm
    anywhere = pl.BlockSpec(memory_space=pl.ANY)
    dma = pltpu.SemaphoreType.DMA
    series = pl.pallas_call(
        functools.partial(kernel, n_sta, n_tm),
        out_shape=jax.ShapeDtypeStruct((SLOTS * PAIRS, lanes), F32),
        in_specs=[anywhere] * (3 + len(consts)),
        out_specs=pl.BlockSpec(memory_space=pltpu.VMEM),
        scratch_shapes=[
            pltpu.SMEM((1,), jnp.int32),
            pltpu.SMEM((SLOTS,), jnp.int32),
            pltpu.VMEM((64, ST, 128), F32),
            pltpu.VMEM((32, ST, 128), F32),
            *[pltpu.VMEM(table.shape, table.dtype) for table in consts],
            pltpu.VMEM((64 * ST, 256), BF16),
            pltpu.VMEM((2 * LIVE_ROWS, ST, 128), F32),
            pltpu.VMEM((256, 512), BF16),
            pltpu.VMEM((256, 512), BF16),
            pltpu.VMEM((2, 2, 2, 128, 128), BF16),
            pltpu.VMEM((2, 4, 32, ST, 128), F32),
            pltpu.VMEM((2, 2, REACH, 2, 128, 128), BF16),
            pltpu.VMEM((2, 2 * PAIRS, FREQ // 2), BF16),
            pltpu.VMEM((2, 4 * PAIRS, FREQ // 2), BF16),
            pltpu.VMEM((2, 4 * PAIRS, 256), F32),
            pltpu.VMEM((n_tm, PAIRS, lanes), BF16),
            pltpu.VMEM((n_tm, 2 * PAIRS, lanes), BF16),
            pltpu.VMEM((n_tm - 1, PAIRS, lanes), BF16),
            pltpu.VMEM((n_tm - 1, 2 * PAIRS, lanes), BF16),
            dma((9,)),
            pltpu.SemaphoreType.REGULAR((n_tm // 2 - 1,)),
            dma((2, 4)),
            dma((2, 2, REACH)),
            dma((2, 2, REACH)),
            dma((n_tm - 1,)),
            dma((n_tm - 1,)),
            dma((n_tm - 1,)),
            dma((n_tm - 1,)),
        ],
        compiler_params=pltpu.CompilerParams(
            collective_id=0, has_side_effects=True, vmem_limit_bytes=VMEM_LIMIT
        ),
    )(x, station_counts, partners.reshape(SLOTS), *consts)
    norm = 1.0 / math.sqrt(2.0 * LENGTH * n_tm)
    return (series * norm).reshape(1, SLOTS, ST, ST, lanes)


def solution(mesh):
    placed = (P("sta", "tm"), P("sta"), P("sta", None))
    return jax.shard_map(
        functools.partial(shards, mesh.shape["sta"], mesh.shape["tm"]),
        mesh=mesh,
        in_specs=placed,
        out_specs=P("sta", None, None, None, "tm"),
        check_vma=False,
    )
```

```python
import functools
import math

import jax
import jax.numpy as jnp
import ml_dtypes
import numpy as np
from jax import lax
from jax.experimental import pallas as pl
from jax.experimental.pallas import tpu as pltpu
from jax.sharding import PartitionSpec as P

MESH = pl.DeviceIdType.MESH
F32 = jnp.float32
BF16 = jnp.bfloat16

ST = 8
FREQ = 4096
LENGTH = 2 * FREQ
BAND = 64
HALF_LAGS = 512
SLOTS = 3
REACH = 3
PAIRS = ST * ST
VMEM_LIMIT = 55100 * 2**10
LIVE_ROWS = 33


def split(table):
    high = table.astype(ml_dtypes.bfloat16)
    low = (table - high.astype(np.float64)).astype(ml_dtypes.bfloat16)
    return np.stack([high, low])


def tables():
    m = np.arange(64)
    q = np.arange(128)
    taper = 0.5 - 0.5 * np.cos(np.arange(LENGTH) * (2.0 * math.pi / LENGTH))
    taper = np.repeat(taper.astype(np.float32).reshape(64, 1, 128), ST, axis=1)
    angle = 2.0 * math.pi * (np.outer(np.arange(LIVE_ROWS), m) % 64) / 64
    first = split(np.kron(np.concatenate([np.cos(angle), -np.sin(angle)]), np.eye(ST)))
    ids = np.arange(32)
    mirrored = np.where(ids == 0, 32, 64 - ids)
    near = 2.0 * math.pi * np.outer(ids, q) / LENGTH
    far = 2.0 * math.pi * np.outer(mirrored, q) / LENGTH
    turn = np.stack([np.cos(near), np.sin(near), np.cos(far), np.sin(far)])
    turn = np.repeat(turn.astype(np.float32)[:, :, None, :], ST, axis=2)
    k = np.arange(BAND)
    angle = 2.0 * math.pi * (np.outer(q, k) % 128) / 128
    cos, sin, none = np.cos(angle), np.sin(angle), np.zeros((128, BAND))
    back_cos, back_sin = cos[:, ::-1], sin[:, ::-1]
    second = np.concatenate(
        [
            np.concatenate([cos, none, -sin, none], axis=1),
            np.concatenate([sin, none, cos, none], axis=1),
            np.concatenate([none, back_cos, none, -back_sin], axis=1),
            np.concatenate([none, back_sin, none, back_cos], axis=1),
        ]
    )
    second = split(second)
    bins = np.concatenate(
        [64 * k[None, :] + ids[:, None], 64 * (63 - k)[None, :] + mirrored[:, None]], axis=1
    )
    angle = math.pi * bins / LENGTH
    shift = np.stack([np.cos(angle), np.sin(angle)]).astype(np.float32)
    shift = np.repeat(shift[:, :, None, :], ST, axis=2)
    order = bins.reshape(-1)
    steps = np.outer(order, 2 * np.arange(HALF_LAGS) + 1) % (2 * LENGTH)
    weight = np.where(order == 0, 1.0, 2.0)
    lag_cos = weight[:, None] * np.cos(math.pi * steps / LENGTH)
    lag_cos = lag_cos.reshape(FREQ, 2, 256).transpose(1, 0, 2).astype(ml_dtypes.bfloat16)
    return taper, first, turn, second, shift, lag_cos


def kernel(
    n_sta,
    n_tm,
    x_hbm,
    counts_hbm,
    partners_hbm,
    tap_hbm,
    first_hbm,
    turn_hbm,
    second_hbm,
    shift_hbm,
    cos_hbm,
    out_ref,
    counts,
    partners,
    xv,
    halo,
    tapv,
    firstv,
    turnv,
    secondv,
    shiftv,
    cosv,
    y,
    u,
    vhi,
    vlo,
    white,
    mine,
    got,
    cross0,
    cross12,
    held,
    part0,
    part12,
    recv0,
    recv12,
    load_sem,
    come,
    halo_sem,
    white_send,
    white_recv,
    p0_send,
    p0_recv,
    p12_send,
    p12_recv,
):
    b = lax.axis_index("sta")
    j = lax.axis_index("tm")
    lanes = 2 * HALF_LAGS // n_tm
    group = n_tm // 2

    barrier = pltpu.get_barrier_semaphore()
    neighbours = [(b, lax.rem(j + 1, n_tm)), (b, lax.rem(j + n_tm - 1, n_tm))]
    odd = lax.rem(b, 2)
    ahead = (lax.rem(b + 2, n_sta), j)
    behind = (lax.rem(b + n_sta - 2, n_sta), j)
    sibling = (b + 1 - 2 * odd, j)
    across = (lax.rem(b + n_sta - 3 + 6 * odd, n_sta), j)
    third = (lax.rem(b + n_sta - 3 + 2 * odd, n_sta), j)
    has_ahead, has_behind = b < n_sta - 2, b >= 2
    sends = [has_behind, (odd == 1) | (b >= 4), has_ahead]
    receives = [has_ahead, (odd == 0) | (b < n_sta - 3), has_ahead]
    has_across = ((odd == 1) & (b < n_sta - 3)) | ((odd == 0) & (b >= 4))
    for peer in neighbours + [sibling]:
        pl.semaphore_signal(barrier, inc=1, device_id=peer, device_id_type=MESH)
    for there, peer in ((has_ahead, ahead), (has_behind, behind), (has_across, across)):
        pl.when(there)(
            functools.partial(
                pl.semaphore_signal, barrier, inc=1, device_id=peer, device_id_type=MESH
            )
        )
    arrivals = 3
    for there in (has_ahead, has_behind, has_across):
        arrivals = arrivals + there.astype(jnp.int32)

    for place in range(REACH):

        @pl.when(jnp.logical_not(receives[place]))
        def _():
            for w in range(2):
                for part in range(2):
                    got[w, part, place] = jnp.zeros((2, 128, 128), BF16)

    def pass_on(step):
        for neighbour in neighbours:
            pl.semaphore_signal(
                come.at[step], inc=1, device_id=neighbour, device_id_type=MESH
            )

    loads = []
    for idx, (src, dst) in enumerate(
        [
            (x_hbm, xv),
            (counts_hbm, counts),
            (partners_hbm, partners),
            (tap_hbm, tapv),
            (first_hbm, firstv),
            (turn_hbm, turnv),
            (second_hbm, secondv),
            (shift_hbm, shiftv),
            (cos_hbm, cosv),
        ]
    ):
        loads.append(pltpu.make_async_copy(src, dst, load_sem.at[idx]))
    for copy in loads[:-1]:
        copy.start()

    def tapered(frames, begin, end):
        frames = (frames * tapv[begin:end]).reshape((end - begin) * ST, 128)
        at = slice(ST * begin, ST * end)
        high = frames.astype(BF16)
        y[at, 0:128] = high
        y[at, 128:256] = (frames - high.astype(F32)).astype(BF16)

    def first_step(begin, end):
        at = slice(ST * begin, ST * end)
        both = jnp.dot(firstv[0, :, at], y[at, :], preferred_element_type=F32)
        return (
            both[:, 0:128]
            + both[:, 128:256]
            + jnp.dot(firstv[1, :, at], y[at, 0:128], preferred_element_type=F32)
        ).reshape(2 * LIVE_ROWS, ST, 128)

    def total(frames):
        return jnp.sum(jnp.sum(frames, axis=0), axis=1, keepdims=True)

    loads[0].wait()
    loads[3].wait()
    frames = xv[...]
    tapered(frames - (total(frames) * (1.0 / LENGTH))[None], 0, 64)
    pl.semaphore_wait(barrier, arrivals)
    halo_copies = []
    for part in range(4):
        rows = pl.ds(8 * part, 8)
        copy = pltpu.make_async_remote_copy(
            src_ref=xv.at[rows],
            dst_ref=halo.at[rows],
            send_sem=halo_sem.at[0, part],
            recv_sem=halo_sem.at[1, part],
            device_id=(b, lax.rem(j + n_tm - 1, n_tm)),
            device_id_type=MESH,
        )
        copy.start()
        halo_copies.append(copy)
    pass_on(0)

    loads[1].wait()
    loads[2].wait()
    station = lax.broadcasted_iota(jnp.int32, (ST, 128), 0)
    live = (station < counts[0]).astype(F32)

    lane = lax.broadcasted_iota(jnp.int32, (ST, 128), 1)
    opposite = jnp.where(lane < 64, (64 - lane) & 63, 191 - lane)

    def by_lane(value, index):
        return jnp.take_along_axis(value, index, axis=1, mode="promise_in_bounds")

    def turned(row):
        re0, im0 = u[row], u[LIVE_ROWS + row]
        re1, im1 = (u[32], u[LIVE_ROWS + 32]) if row == 0 else (re0, im0)
        c0, s0, c1, s1 = turnv[0, row], turnv[1, row], turnv[2, row], turnv[3, row]
        return (
            re0 * c0 + im0 * s0,
            im0 * c0 - re0 * s0,
            re1 * c1 - im1 * s1,
            -(im1 * c1 + re1 * s1),
        )

    def mirrored_bins(value):
        first = jnp.where(lane == 0, 0.0, by_lane(value[0], opposite))
        return jnp.concatenate([first[None], pltpu.roll(value[1:], 64, 2)])

    def second_step(w, rest=None):
        for i in range(16):
            pair = zip(turned(2 * i), turned(2 * i + 1))
            for block, (upper, lower) in enumerate(pair):
                v = jnp.concatenate([upper, lower], axis=0)
                high = v.astype(BF16)
                vhi[16 * i : 16 * i + 16, 128 * block : 128 * block + 128] = high
                vlo[16 * i : 16 * i + 16, 128 * block : 128 * block + 128] = (
                    v - high.astype(F32)
                ).astype(BF16)
        spec = (
            jnp.dot(vhi[...], secondv[0], preferred_element_type=F32)
            + jnp.dot(vlo[...], secondv[0], preferred_element_type=F32)
            + jnp.dot(vhi[...], secondv[1], preferred_element_type=F32)
        )
        re = spec[:, 0:128].reshape(32, ST, 128)
        im = spec[:, 128:256].reshape(32, ST, 128)
        if rest is not None:
            rest = jnp.where(lane == 0, rest * (LENGTH / 4), 0.0)
            re = jnp.concatenate([(re[0] - 2.0 * rest)[None], (re[1] + rest)[None], re[2:]])
        energy = jnp.sum(re * re + im * im, axis=0)
        energy = (energy + by_lane(energy, 127 - lane)) * (1.0 / BAND)
        scale = live / jnp.sqrt(energy + 1e-06)
        re = (re * scale[None]).reshape(2, 128, 128).astype(BF16)
        im = (im * scale[None]).reshape(2, 128, 128).astype(BF16)
        for part in range(2):
            white[w, part, 0] = re[part]
            white[w, part, 1] = im[part]

    def shifted(w):
        re = white[w, :, 0].astype(F32).reshape(32, ST, 128)
        im = white[w, :, 1].astype(F32).reshape(32, ST, 128)
        left = (re * shiftv[0] + im * shiftv[1], im * shiftv[0] - re * shiftv[1])
        for c in range(2):
            mine[w, c] = left[c]
            mine[w, 2 + c] = mirrored_bins(left[c])

    def start_white(w, part, place, source, to):
        copy = pltpu.make_async_remote_copy(
            src_ref=source,
            dst_ref=got.at[w, part, place],
            send_sem=white_send.at[w, part, place],
            recv_sem=white_recv.at[w, part, place],
            device_id=to,
            device_id_type=MESH,
        )
        pl.when(sends[place])(copy.start)
        return copy

    def send_near(w):
        return [[start_white(w, part, 0, white.at[w, part], behind)] for part in range(2)]

    def send_far(w, copies):
        for part in range(2):
            copies[part].append(start_white(w, part, 1, white.at[w, part], third))

    def hand_on(w, part, copies):
        pl.when(receives[0])(copies[part][0].wait_recv)
        copies[part].append(start_white(w, part, 2, got.at[w, part, 0], sibling))

    def arrive(copies):
        for place in (1, 2):
            pl.when(receives[place])(copies[place].wait_recv)

    loads[4].wait()
    u[...] = first_step(0, 64)
    loads[5].wait()
    loads[6].wait()
    second_step(0)
    loads[-1].start()
    sent0 = send_near(0)
    send_far(0, sent0)
    pl.semaphore_wait(come.at[0], 2)
    pass_on(1)
    loads[7].wait()
    shifted(0)
    frames = xv[32:64]
    mean = total(frames) * (2.0 / LENGTH)
    tapered(frames - mean[None], 0, 32)
    u[...] = first_step(0, 32)
    for copy in halo_copies:
        copy.wait()
    inside = (j < n_tm - 1).astype(F32)
    frames = halo[...] * inside - mean[None]
    tapered(frames, 32, 64)
    u[...] += first_step(32, 64)
    second_step(1, total(frames) * (1.0 / LENGTH))
    sent1 = send_near(1)
    pl.semaphore_wait(come.at[1], 2)
    pass_on(2)
    shifted(1)

    def cross_pair(others, cross, slots, windows, part, i):
        right = others(part, slice(16 * i, 16 * i + 16), windows)
        for half in range(2):
            row = 16 * part + 2 * i + half
            at = slice(128 * (row - 16 * part), 128 * (row - 16 * part) + 128)
            own = slice(8 * half, 8 * half + 8)
            terms = []
            for slot in range(slots):
                terms.append([])
                for pair in right[slot]:
                    values = [value[own] for value in pair]
                    if row == 0:
                        values += [by_lane(value, opposite) for value in values]
                    else:
                        values += [pltpu.roll(value, 64, 1) for value in values]
                    terms[slot].append(values)
            for s in range(0, ST, 2):
                kept = [[], []]
                for t in (s, s + 1):
                    left = [
                        [
                            jnp.broadcast_to(mine[w, c, row, t : t + 1, :], (ST, 128))
                            for c in range(4)
                        ]
                        for w in windows
                    ]
                    for slot in range(slots):
                        re, im = None, None
                        for mine_values, values in zip(left, terms[slot]):
                            a_re, a_im, back_re, back_im = mine_values
                            o_re, o_im, other_re, other_im = values
                            new_re = a_re * o_re + a_im * o_im
                            new_im = back_im * other_re - back_re * other_im
                            re = new_re if re is None else re + new_re
                            im = new_im if im is None else im + new_im
                        kept[0].append(re - im)
                        kept[1].append(re + im)
                for slot in range(slots):
                    for sign in range(2):
                        at_rows = pl.ds((sign * slots + slot) * PAIRS + s * ST, 16)
                        cross[part, at_rows, at] = jnp.concatenate(
                            [kept[sign][slot], kept[sign][slots + slot]], axis=0
                        ).astype(BF16)

    def cross_terms(others, cross, slots, windows, part):
        for i in range(8):
            cross_pair(others, cross, slots, windows, part, i)

    half_bins = FREQ // 2

    def lag_sums(cross, half, part):
        at = slice(half_bins * part, half_bins * part + half_bins)
        return jnp.dot(cross[part], cosv[half, at, :], preferred_element_type=F32)

    def all_sums(cross, half):
        return lag_sums(cross, half, 0) + lag_sums(cross, half, 1)

    def keep_part(sums, half, part):
        rows = sums.shape[0] // 2
        even = (lax.broadcasted_iota(jnp.int32, (rows, 256), 1) & 1) == 0
        minus, plus = sums[:rows], sums[rows:]
        later = jnp.where(even, minus, plus).astype(BF16)
        earlier = jnp.where(even, plus, minus).astype(BF16)
        for e in range(n_tm // 4):
            at = slice(lanes * e, lanes * e + lanes)
            block = half * (n_tm // 4) + e
            part[group + block] = later[:, at]
            part[group - 1 - block] = earlier[:, at]

    def send_part(part, recv, send_sem, recv_sem):
        copies = []
        for d in sorted(range(1, n_tm), key=lambda d: -min(d, n_tm - d)):
            to = lax.rem(j + d, n_tm)
            copy = pltpu.make_async_remote_copy(
                src_ref=part.at[to],
                dst_ref=recv.at[d - 1],
                send_sem=send_sem.at[d - 1],
                recv_sem=recv_sem.at[d - 1],
                device_id=(b, to),
                device_id_type=MESH,
            )
            copy.start()
            copies.append((d, copy))
        return copies

    def own_rows(part, rows, windows):
        return [[[white[w, part, c, rows, :].astype(F32) for c in range(2)] for w in windows]]

    cross_terms(own_rows, cross0, 1, (0, 1), 0)
    send_far(1, sent1)
    hand_on(0, 0, sent0)
    hand_on(0, 1, sent0)
    cross_terms(own_rows, cross0, 1, (0, 1), 1)
    loads[-1].wait()
    for half in range(2):
        keep_part(all_sums(cross0, half), half, part0)
    pl.semaphore_wait(come.at[2], 2)
    terms0 = send_part(part0, recv0, p0_send, p0_recv)

    offsets = (2, 1 + 2 * odd, 3 - 2 * odd)
    takes = [
        [(partners[slot] == b + offset).astype(F32) for offset in offsets]
        for slot in range(1, SLOTS)
    ]

    def chosen(part, rows, windows):
        slots = [[] for _ in takes]
        for w in windows:
            pairs = [[] for _ in takes]
            for c in range(2):
                values = [got[w, part, d, c, rows, :].astype(F32) for d in range(REACH)]
                for pair, take in zip(pairs, takes):
                    pair.append(values[0] * take[0] + values[1] * take[1] + values[2] * take[2])
            for slot, pair in zip(slots, pairs):
                slot.append(pair)
        return slots

    for part in range(2):
        arrive(sent0[part])
        cross_terms(chosen, cross12, SLOTS - 1, (0,), part)
    hand_on(1, 0, sent1)
    hand_on(1, 1, sent1)
    for half in range(2):
        held[half] = all_sums(cross12, half)
    for part in range(2):
        arrive(sent1[part])
        if part == 1:
            for half in range(2):
                held[half] += lag_sums(cross12, half, 0)
        cross_terms(chosen, cross12, SLOTS - 1, (1,), part)
    for half in range(2):
        keep_part(held[half] + lag_sums(cross12, half, 1), half, part12)
    terms12 = send_part(part12, recv12, p12_send, p12_recv)

    at = lax.broadcasted_iota(jnp.int32, (ST, lanes), 1)
    at = jnp.where(j >= group, at, lanes - 1 - at)

    def finish(part, recv, copies):
        series = part[j].astype(F32)
        for d, copy in reversed(copies):
            copy.wait()
            series = series + recv[d - 1].astype(F32)
        blocks = [by_lane(series[r : r + ST], at) for r in range(0, series.shape[0], ST)]
        return jnp.concatenate(blocks, axis=0)

    for copies in sent0 + sent1:
        for place, copy in enumerate(copies):
            pl.when(sends[place])(copy.wait_send)
    own = finish(part0, recv0, terms0)
    pair = lax.broadcasted_iota(jnp.int32, (PAIRS, lanes), 0)
    own = jnp.where((pair >> 3) == (pair & 7), 0.0, own)
    out_ref[0:PAIRS, :] = own
    out_ref[PAIRS : SLOTS * PAIRS, :] = finish(part12, recv12, terms12)


def shards(n_sta, n_tm, traces, station_counts, partners):
    x = traces.reshape(ST, 64, 128).transpose(1, 0, 2)
    consts = [jnp.asarray(table) for table in tables()]
    lanes = 2 * HALF_LAGS // n_tm
    anywhere = pl.BlockSpec(memory_space=pl.ANY)
    dma = pltpu.SemaphoreType.DMA
    series = pl.pallas_call(
        functools.partial(kernel, n_sta, n_tm),
        out_shape=jax.ShapeDtypeStruct((SLOTS * PAIRS, lanes), F32),
        in_specs=[anywhere] * (3 + len(consts)),
        out_specs=pl.BlockSpec(memory_space=pltpu.VMEM),
        scratch_shapes=[
            pltpu.SMEM((1,), jnp.int32),
            pltpu.SMEM((SLOTS,), jnp.int32),
            pltpu.VMEM((64, ST, 128), F32),
            pltpu.VMEM((32, ST, 128), F32),
            *[pltpu.VMEM(table.shape, table.dtype) for table in consts],
            pltpu.VMEM((64 * ST, 256), BF16),
            pltpu.VMEM((2 * LIVE_ROWS, ST, 128), F32),
            pltpu.VMEM((256, 512), BF16),
            pltpu.VMEM((256, 512), BF16),
            pltpu.VMEM((2, 2, 2, 128, 128), BF16),
            pltpu.VMEM((2, 4, 32, ST, 128), F32),
            pltpu.VMEM((2, 2, REACH, 2, 128, 128), BF16),
            pltpu.VMEM((2, 2 * PAIRS, FREQ // 2), BF16),
            pltpu.VMEM((2, 4 * PAIRS, FREQ // 2), BF16),
            pltpu.VMEM((2, 4 * PAIRS, 256), F32),
            pltpu.VMEM((n_tm, PAIRS, lanes), BF16),
            pltpu.VMEM((n_tm, 2 * PAIRS, lanes), BF16),
            pltpu.VMEM((n_tm - 1, PAIRS, lanes), BF16),
            pltpu.VMEM((n_tm - 1, 2 * PAIRS, lanes), BF16),
            dma((9,)),
            pltpu.SemaphoreType.REGULAR((n_tm // 2 - 1,)),
            dma((2, 4)),
            dma((2, 2, REACH)),
            dma((2, 2, REACH)),
            dma((n_tm - 1,)),
            dma((n_tm - 1,)),
            dma((n_tm - 1,)),
            dma((n_tm - 1,)),
        ],
        compiler_params=pltpu.CompilerParams(
            collective_id=0, has_side_effects=True, vmem_limit_bytes=VMEM_LIMIT
        ),
    )(x, station_counts, partners.reshape(SLOTS), *consts)
    norm = 1.0 / math.sqrt(2.0 * LENGTH * n_tm)
    return (series * norm).reshape(1, SLOTS, ST, ST, lanes)


def solution(mesh):
    placed = (P("sta", "tm"), P("sta"), P("sta", None))
    return jax.shard_map(
        functools.partial(shards, mesh.shape["sta"], mesh.shape["tm"]),
        mesh=mesh,
        in_specs=placed,
        out_specs=P("sta", None, None, None, "tm"),
        check_vma=False,
    )
```
